32 devices in a mesh: gx: 8 (over y, x, core), gy: 4 (over z).
Axes of the slice: x: 2, y: 2, z: 4, core: 2. Of those that a mesh axis runs over, the one named last changes fastest.
Arguments:
- populations: float32 [19, 128, 64, 128], P(None, 'gx', 'gy'), may hold values from 0.5 to 1.5
- coarse_state: float32 [4, 64, 32, 64], P(None, 'gx', 'gy'), may hold values from -3 to 3
- window_shift: int32 [1], replicated, may hold values from 1 to 7
- inflow: float32 [3], replicated, may hold values from -0.2 to 0.2
- relaxation: float32 [1], replicated, may hold values from 1 to 1.7
- positions: float32 [512, 3, 642], P(('gx', 'gy')), may hold values from 0.25 to 6.75
- rest_shape: float32 [3, 642], replicated, may hold values from -6 to 6
- stiffness: float32 [512], P(('gx', 'gy')), may hold values from 0.1 to 1
- cell_owner: int32 [512, 1], P(('gx', 'gy')), may hold values from 0 to 7; in each aligned block of 16 rows (0 to 15, 16 to 31, ...) at most 4 rows name the same one
- cell_block: int32 [512], P(('gx', 'gy')), may hold values from 0 to 63
- triangles: int32 [1280, 3], replicated, may hold values from 0 to 641, as said below
Outputs:
- flow: float32 [19, 128, 64, 128], P(None, 'gx', 'gy')
- cell_velocity: float32 [512, 3, 642], P(('gx', 'gy'))
The draws below stay inside these ranges and needn't reach their ends.
Inputs may be any that keep to these rules, and one draw needn't show every extreme that they name: `triangles`: each triangle names three different vertices. `cell_owner`: among the cells of one device, no owner is named by more than 4 cells.
All inputs are finite; a program needn't handle non-finite values.
Results may differ from the reference program's by a relative error of at most 0.0003.
Values sent between devices are 32-bit elements; how exact they have to be, the bound alone decides.
A program may use at most 128 MiB of HBM per device.

```python
import math
import jax
import jax.numpy as jnp
import numpy as np
from jax import lax

Q = 19
BS = 8
CX = 16
CY = 16
CZ = 128
V = 642
NTRI = 1280
CELLS_DEV = 16
CAP = 4
NB_DEV = 64
NX = 128
NY = 64
NZ = 128
CELLS = 512
N_GX = 8
N_GY = 4


def draw_triangles(key, part):
    first_key, second_key, third_key = jax.random.split(jax.random.fold_in(key, 17), 3)
    first = jax.random.randint(first_key, (NTRI,), 0, V)
    offset_near = jax.random.randint(second_key, (NTRI,), 1, V // 2)
    offset_far = jax.random.randint(third_key, (NTRI,), V // 2, V)
    return jnp.stack([first, (first + offset_near) % V, (first + offset_far) % V], 1).astype(jnp.int32)


def touch_ends(entries, key, least, largest):
    longest = entries.shape.index(max(entries.shape))
    spots = []
    for shift in (0, 1):
        where = [jax.random.randint(jax.random.fold_in(key, axis), (), 0, length) for axis, length in enumerate(entries.shape)]
        where[longest] = (where[longest] + shift) % entries.shape[longest]
        spots.append(tuple(where))
    return entries.at[spots[0]].set(least).at[spots[1]].set(largest)


def steps_of(rng, shape, shards, smallest, largest):
    def one(dim, shards_of):
        steps = jax.random.uniform(jax.random.fold_in(jax.random.fold_in(rng, 6), dim), (shards_of,), jnp.float32, smallest / len(shards), largest / len(shards))
        return jnp.repeat(jnp.exp(steps), shape[dim] // shards_of).reshape((-1,) + (1,) * (len(shape) - dim - 1))

    gain = one(*shards[0])
    for cut in shards[1:]:
        gain = gain * one(*cut)
    return gain


def deal_out(key, own, number, rows, number_of, top, bound, skew):
    sequence = jax.random.permutation(key, number_of)
    crowded, common = shares(number_of, rows * top, bound, skew, True), shares(number_of, rows * top, bound, skew, False)
    places = jnp.arange(number_of)

    def named(lengths, turn):
        used = int((lengths > 0).sum())
        fixed = max(1, used // 4)
        shifted = fixed + (places - fixed + turn * (used - fixed)) % max(1, number_of - fixed)
        return jnp.zeros((number_of,), jnp.int32).at[sequence[jnp.where(places < fixed, places, shifted)]].set(jnp.asarray(lengths, jnp.int32))

    lengths = jnp.where(number % 4 == 0, named(crowded, number // 4), named(common, number - number // 4 - 1))
    mixed = jax.random.permutation(jax.random.fold_in(own, 3), number_of)
    source_of, sink = mixed[0:number_of // 2 * 2:2], mixed[1:number_of // 2 * 2:2]
    slack = jnp.minimum(lengths[source_of] - 1, bound - lengths[sink]) // 2
    slack = jnp.where((source_of == sequence[0]) | (sink == sequence[0]) | (lengths[sink] == 0), 0, jnp.maximum(slack, 0))
    shifted = jax.random.randint(jax.random.fold_in(own, 4), (number_of // 2,), 0, 1 << 20) % (slack + 1)
    lengths = lengths.at[source_of].add(-shifted).at[sink].add(shifted)
    items = jnp.searchsorted(jnp.cumsum(lengths), jnp.arange(rows * top), side="right").astype(jnp.int32)
    grid = items.reshape(top, rows).T
    grid = grid[jax.random.permutation(jax.random.fold_in(own, 1), rows)]
    turn = jax.random.randint(jax.random.fold_in(own, 2), (rows, 1), 0, top)
    return jnp.take_along_axis(grid, (jnp.arange(top)[None, :] + turn) % top, axis=1)


def shares(number_of, total, limit, skew, full):
    portions = [(1 << 20) // math.isqrt(rank ** skew) + 1 for rank in range(1, number_of + 1)]
    largest = limit if full else min(limit, max(-(-total // number_of), total * portions[0] // sum(portions)))
    least = 1 if total - largest >= number_of - 1 else 0
    holding, rest = [largest] + [least] * (number_of - 1), total - largest - least * (number_of - 1)
    while rest > 0:
        free = [i for i in range(1, number_of) if holding[i] < largest] or [i for i in range(1, number_of) if holding[i] < limit]
        whole, budget = sum([portions[i] for i in free]), rest
        for i in free:
            more = min(limit - holding[i], max(1, budget * portions[i] // whole), rest)
            holding[i] = holding[i] + more
            rest = rest - more
    return np.array(holding)


def bell_draw(stream_key, dims, scale, bound, cuts=(), kind=jnp.bfloat16):
    gain = steps_of(stream_key, dims, cuts, -0.22, 0.18) if cuts else 1.0
    entries = jax.random.normal(stream_key, dims, jnp.float32) * scale * gain
    return jnp.minimum(jnp.maximum(entries, -bound), bound).astype(kind)


def setup_inputs(seed: int = 0) -> dict:
    streams_of = jax.random.split(jax.random.key(seed), 12)
    populations = jnp.clip(1.0 + 0.1 * jax.random.normal(streams_of[0], (Q, NX, NY, NZ), jnp.float32), 0.5, 1.5)
    coarse_state = bell_draw(streams_of[1], (4, NX // 2, NY // 2, NZ // 2), 1.0, 3.0, ((1, 8), (2, 4)), jnp.float32)
    window_shift = jax.random.randint(streams_of[2], (1,), 1, N_GX).astype(jnp.int32)
    inflow = bell_draw(streams_of[3], (3,), 0.05, 0.2, (), jnp.float32)
    relaxation = jnp.clip(jax.random.uniform(streams_of[4], (1,), jnp.float32, 1.0, 1.7), 1.0, 1.7)
    positions = jnp.clip(0.25 + 6.5 * jax.random.uniform(streams_of[5], (CELLS, 3, V), jnp.float32) ** steps_of(streams_of[5], (CELLS, 3, V), ((0, 32),), -0.2, 0.2), 0.25, 6.75)
    rest_shape = bell_draw(streams_of[6], (3, V), 1.5, 6.0, (), jnp.float32)
    stiffness = jnp.clip(jnp.exp(math.log(1.0) - 2.3025851 * jax.random.uniform(streams_of[7], (CELLS,), jnp.float32) ** steps_of(streams_of[7], (CELLS,), ((0, 32),), -0.2, 0.2)), 0.1, 1.0)
    cell_owner_keys = jax.random.split(jax.random.fold_in(streams_of[8], 1), CELLS // CELLS_DEV)
    cell_owner_turns = jax.random.permutation(jax.random.fold_in(streams_of[8], 3), CELLS // CELLS_DEV)
    cell_owner = jax.vmap(lambda own, number: deal_out(jax.random.fold_in(streams_of[8], 2), own, number, CELLS_DEV, N_GX, 1, CAP, 2))(cell_owner_keys, cell_owner_turns).reshape((CELLS, 1))
    cell_block = touch_ends(jax.random.randint(streams_of[9], (CELLS,), 0, NB_DEV), jax.random.fold_in(streams_of[9], 1), 0, NB_DEV - 1).astype(jnp.int32)
    triangles = draw_triangles(jax.random.fold_in(streams_of[11], 71), 0)
    return dict(populations=populations, coarse_state=coarse_state, window_shift=window_shift, inflow=inflow, relaxation=relaxation, positions=positions, rest_shape=rest_shape, stiffness=stiffness, cell_owner=cell_owner, cell_block=cell_block, triangles=triangles)


LATTICE = ((0, 0, 0), (1, 0, 0), (-1, 0, 0), (0, 1, 0), (0, -1, 0), (0, 0, 1), (0, 0, -1),
           (1, 1, 0), (-1, -1, 0), (1, -1, 0), (-1, 1, 0), (1, 0, 1), (-1, 0, -1), (1, 0, -1), (-1, 0, 1),
           (0, 1, 1), (0, -1, -1), (0, 1, -1), (0, -1, 1))
WEIGHTS = (1.0 / 3.0,) + (1.0 / 18.0,) * 6 + (1.0 / 36.0,) * 12
COUPLING = 0.001
VELOCITY_UNIT = 20.0
HIGHEST = lax.Precision.HIGHEST


def equilibrium(density, velocity):
    square = velocity[0] * velocity[0] + velocity[1] * velocity[1] + velocity[2] * velocity[2]
    rows = []
    for along_x, along_y, along_z in LATTICE:
        project = along_x * velocity[0] + along_y * velocity[1] + along_z * velocity[2]
        rows.append(density * (1.0 + 3.0 * project + 4.5 * project * project - 1.5 * square))
    return jnp.stack(rows)


def moments(state):
    density = WEIGHTS[0] * state[0]
    for column in range(1, 19):
        density = density + WEIGHTS[column] * state[column]
    momentum = []
    for axis_id in range(3):
        total = jnp.zeros_like(density)
        for column in range(19):
            if LATTICE[column][axis_id] != 0:
                total = total + (WEIGHTS[column] * LATTICE[column][axis_id]) * state[column]
        momentum.append(total)
    return density, jnp.stack(momentum) / density


def hat_weights(point):
    nodes = jnp.arange(BS).astype(point.dtype)
    factors = [jnp.maximum(0.0, 1.0 - jnp.abs(point[axis_id][:, None] - nodes[None, :])) for axis_id in range(3)]
    joined = factors[0][:, :, None, None] * factors[1][:, None, :, None] * factors[2][:, None, None, :]
    return joined.reshape(point.shape[1], BS * BS * BS)


def laplacian(triangles, count):
    vertices = jnp.arange(count, dtype=jnp.int32)
    ends = [(triangles[:, corner][:, None] == vertices[None, :]).astype(jnp.float32) for corner in range(3)]
    total = jnp.zeros((count, count), jnp.float32)
    for first, second in ((0, 1), (1, 2), (2, 0)):
        edge = ends[second] - ends[first]
        total = total + jnp.dot(edge.T, edge, precision=HIGHEST)
    return total


def lattice_step(state, force, omega, ghost):
    density, velocity = moments(state)
    target = equilibrium(density, velocity)
    extent_x, extent_y = state.shape[1], state.shape[2]
    places_x = jnp.arange(extent_x + 2)
    places_y = jnp.arange(extent_y + 2)
    outside = ((places_x == 0) | (places_x == extent_x + 1))[:, None] | ((places_y == 0) | (places_y == extent_y + 1))[None, :]
    rows = []
    for column in range(19):
        along_x, along_y, along_z = LATTICE[column]
        push = 3.0 * (along_x * force[0] + along_y * force[1] + along_z * force[2])
        post = state[column] - omega * (state[column] - target[column]) + push
        padded = jnp.pad(post, ((1, 1), (1, 1), (0, 0)))
        padded = jnp.where(outside[:, :, None], ghost[column], padded)
        moved = padded[1 - along_x:1 - along_x + extent_x, 1 - along_y:1 - along_y + extent_y, :]
        rows.append(jnp.roll(moved, along_z, axis=2))
    return jnp.stack(rows)


def reference(populations, coarse_state, window_shift, inflow, relaxation, positions, rest_shape, stiffness, cell_owner, cell_block, triangles):
    extent_x = populations.shape[1]
    shift_rows = (window_shift[0] * CX).astype(jnp.int32)
    moved = jnp.roll(populations, -shift_rows, axis=1)
    coarse = jnp.repeat(jnp.repeat(jnp.repeat(coarse_state, 2, 1), 2, 2), 2, 3)
    fill = equilibrium(1.0 + 0.1 * coarse[0], 0.05 * coarse[1:4])
    entering = jnp.arange(extent_x, dtype=jnp.int32) + shift_rows >= extent_x
    state = jnp.where(entering[None, :, None, None], fill, moved)

    lap = laplacian(triangles, positions.shape[2])
    shape_gap = positions - rest_shape[None]
    forces = -stiffness[:, None, None] * jnp.einsum("cdv,vw->cdw", shape_gap, lap, precision=HIGHEST)

    cell_count = positions.shape[0]
    rows_y = ((jnp.arange(cell_count, dtype=jnp.int32) // CELLS_DEV) % N_GY).astype(jnp.int32)
    blocks_y = CY // BS
    blocks_z = CZ // BS
    zero = jnp.zeros((), jnp.int32)

    def anchor(owner, block, row):
        start_x = (owner * CX + block // (blocks_y * blocks_z) * BS).astype(jnp.int32)
        start_y = (row * CY + block // blocks_z % blocks_y * BS).astype(jnp.int32)
        start_z = (block % blocks_z * BS).astype(jnp.int32)
        return start_x, start_y, start_z

    def spread(field, item):
        point, push, owner, block, row = item
        local = jnp.dot(push, hat_weights(point), precision=HIGHEST).reshape(3, BS, BS, BS)
        start_x, start_y, start_z = anchor(owner, block, row)
        current = lax.dynamic_slice(field, (zero, start_x, start_y, start_z), (3, BS, BS, BS))
        return lax.dynamic_update_slice(field, current + local, (zero, start_x, start_y, start_z)), None

    empty = jnp.zeros((3,) + populations.shape[1:], jnp.float32)
    field, _ = lax.scan(spread, empty, (positions, forces, cell_owner[:, 0], cell_block, rows_y))
    force = COUPLING * field

    ghost = equilibrium(1.0, inflow)
    omega = relaxation[0]
    for repeat in range(2):
        state = lattice_step(state, force, omega, ghost)
    _, velocity = moments(state)

    def sample(carry, item):
        point, owner, block, row = item
        start_x, start_y, start_z = anchor(owner, block, row)
        local = lax.dynamic_slice(velocity, (zero, start_x, start_y, start_z), (3, BS, BS, BS)).reshape(3, BS * BS * BS)
        return carry, VELOCITY_UNIT * jnp.dot(local, hat_weights(point).T, precision=HIGHEST)

    _, cell_velocity = lax.scan(sample, zero, (positions, cell_owner[:, 0], cell_block, rows_y))
    return state, cell_velocity
```

```python
import functools
import jax
import jax.numpy as jnp
from jax import lax
from jax.experimental import pallas as pl
from jax.experimental.pallas import tpu as pltpu
from jax.sharding import PartitionSpec as P

BS = 8
LATTICE = (
    (0, 0, 0),
    (1, 0, 0),
    (-1, 0, 0),
    (0, 1, 0),
    (0, -1, 0),
    (0, 0, 1),
    (0, 0, -1),
    (1, 1, 0),
    (-1, -1, 0),
    (1, -1, 0),
    (-1, 1, 0),
    (1, 0, 1),
    (-1, 0, -1),
    (1, 0, -1),
    (-1, 0, 1),
    (0, 1, 1),
    (0, -1, -1),
    (0, 1, -1),
    (0, -1, 1),
)
Q = len(LATTICE)
COUPLING = 0.001
VELOCITY_UNIT = 20.0
HIGHEST = lax.Precision.HIGHEST
MESH = pl.DeviceIdType.MESH
PAD = 8
FACES = ((1, 0), (-1, 0), (0, 1), (0, -1), (1, 1), (-1, -1), (1, -1), (-1, 1))


def columns_along(dx, dy):
    return [
        q
        for q, (cx, cy, _) in enumerate(LATTICE)
        if (dx == 0 or cx == dx) and (dy == 0 or cy == dy)
    ]


def halves(x):
    high = x.astype(jnp.bfloat16)
    low = (x - high.astype(jnp.float32)).astype(jnp.bfloat16)
    return high, low


def rows_dot(a, b):
    return lax.dot_general(a, b, (((1,), (1,)), ((), ())), preferred_element_type=jnp.float32)


def plain_dot(a, b):
    return lax.dot_general(a, b, (((1,), (0,)), ((), ())), preferred_element_type=jnp.float32)


def hats(pos_ref, c):
    nodes = lax.broadcasted_iota(jnp.int32, (BS, pos_ref.shape[2]), 0).astype(jnp.float32)
    return [
        jnp.maximum(0.0, 1.0 - jnp.abs(pos_ref[d, pl.ds(c, 1), :] - nodes)) for d in range(3)
    ]


def spread_kernel(
    span, cap, pos_ref, rest_ref, stiff_ref, owner_ref, block_ref, tri_ref,
    out_ref, slot_ref, force_ref, count_ref,
):
    _, cells, count = pos_ref.shape
    tri = tri_ref[...]
    vertices = lax.broadcasted_iota(jnp.int32, (tri.shape[0], count), 1)
    hit = (tri[:, 0:1] == vertices) | (tri[:, 1:2] == vertices) | (tri[:, 2:3] == vertices)
    member = jnp.where(hit, 1.0, 0.0)
    degree = jnp.sum(member, axis=0, keepdims=True)
    member = member.astype(jnp.bfloat16)
    gap = jnp.concatenate([pos_ref[d] - rest_ref[d : d + 1, :] for d in range(3)], axis=0)
    high, low = halves(gap)
    each = rows_dot(high, member) + rows_dot(low, member)
    high, low = halves(each)
    back = plain_dot(high, member) + plain_dot(low, member)
    force_ref[...] = (back - 3.0 * degree * gap).reshape(3, cells, count)
    out_ref[...] = jnp.zeros_like(out_ref)
    for o in range(span):
        count_ref[o] = 0
    lanes = lax.broadcasted_iota(jnp.int32, (BS, out_ref.shape[1]), 1)
    used = 3 * BS * BS
    spare = jnp.zeros((out_ref.shape[1] - used, count), jnp.bfloat16)

    def one(c, carry):
        wx, wy, wz = hats(pos_ref, c)
        rows = []
        for d in range(3):
            push = force_ref[d, pl.ds(c, 1), :] * stiff_ref[c]
            for x in range(BS):
                rows.append((push * wx[x : x + 1]) * wy)
        high, low = halves(jnp.concatenate(rows, axis=0))
        weights = jnp.concatenate(halves(wz), axis=0)
        first = rows_dot(weights, jnp.concatenate([high, spare], axis=0))
        second = rows_dot(weights, jnp.concatenate([low, spare], axis=0))
        block = first[:BS] + first[BS:] + second[:BS]
        tag = (block_ref[c] + 1).astype(jnp.float32)
        owner = owner_ref[c]
        rank = count_ref[owner]
        count_ref[owner] = rank + 1
        slot = owner * cap + rank
        slot_ref[c] = slot
        out_ref[pl.ds(pl.multiple_of(slot * BS, BS), BS), :] = jnp.where(lanes < used, block, tag)
        return carry

    lax.fori_loop(0, cells, one, 0)


def field_kernel(arrived_ref, coarse_ref, field_ref, up_ref, hit_ref):
    _, extent_x, extent_y, extent_z = field_ref.shape
    used = 3 * BS * BS
    slots, width = hit_ref.shape
    tag = arrived_ref[:, used : used + 1]
    row = lax.broadcasted_iota(jnp.int32, (slots, width), 0)
    col = lax.broadcasted_iota(jnp.int32, (slots, width), 1)
    same = (tag - 1.0 == (col // BS).astype(jnp.float32)) & (row % BS == col % BS)
    hit = jnp.where(same, 1.0, 0.0).astype(jnp.bfloat16)
    hit_ref[...] = hit
    high, low = halves(arrived_ref[...].T)
    placed = COUPLING * (plain_dot(high, hit) + plain_dot(low, hit))
    across = extent_y // BS
    for bx in range(extent_x // BS):
        for by in range(across):
            c = bx * across + by
            for d in range(3):
                part = placed[d * BS * BS : (d + 1) * BS * BS, c * extent_z : (c + 1) * extent_z]
                field_ref[d, bx * BS : (bx + 1) * BS, by * BS : (by + 1) * BS, :] = part.reshape(
                    BS, BS, extent_z
                )
    coarse = coarse_ref[...]
    rows, depth = coarse.shape
    pick_z = jnp.where(
        lax.broadcasted_iota(jnp.int32, (depth, extent_z), 1) // 2
        == lax.broadcasted_iota(jnp.int32, (depth, extent_z), 0),
        1.0,
        0.0,
    )
    pick_y = jnp.where(
        lax.broadcasted_iota(jnp.int32, (2 * rows, rows), 0) // 2
        == lax.broadcasted_iota(jnp.int32, (2 * rows, rows), 1),
        1.0,
        0.0,
    )
    along = jnp.dot(coarse, pick_z, precision=HIGHEST, preferred_element_type=jnp.float32)
    wide = jnp.dot(pick_y, along, precision=HIGHEST, preferred_element_type=jnp.float32)
    up_ref[...] = wide.reshape(up_ref.shape)


def moments(g):
    axis_sum = (g[1] + g[2]) + (g[3] + g[4]) + (g[5] + g[6])
    edge_sum = g[7]
    for q in range(8, Q):
        edge_sum = edge_sum + g[q]
    density = g[0] * (1.0 / 3.0) + axis_sum * (1.0 / 18.0) + edge_sum * (1.0 / 36.0)
    pair = {q: g[q] - g[q + 1] for q in range(1, Q, 2)}
    inverse = 1.0 / density
    velocity = []
    for d in range(3):
        axis, edge = None, None
        for q in range(1, Q, 2):
            sign = LATTICE[q][d]
            if sign == 0:
                continue
            term = pair[q] if sign > 0 else -pair[q]
            if q < 7:
                axis = term
            else:
                edge = term if edge is None else edge + term
        velocity.append((axis * (1.0 / 18.0) + edge * (1.0 / 36.0)) * inverse)
    return density, velocity


def along(c, v):
    total = None
    for d in range(3):
        if c[d] != 0:
            term = v[d] if c[d] > 0 else -v[d]
            total = term if total is None else total + term
    return total


def collide(g, density, velocity, force, omega):
    square = velocity[0] * velocity[0] + velocity[1] * velocity[1] + velocity[2] * velocity[2]
    base = 1.0 - 1.5 * square
    rated = omega * density
    keep = 1.0 - omega
    post = [keep * g[0] + rated * base]
    for q in range(1, Q, 2):
        project = along(LATTICE[q], velocity)
        even = rated * (base + 4.5 * (project * project))
        odd = 3.0 * (rated * project + along(LATTICE[q], force))
        post.append(keep * g[q] + (even + odd))
        post.append(keep * g[q + 1] + (even - odd))
    return post


def flow_kernel(
    span_x, span_y, state_ref, field_ref, up_ref, hit_ref, par_ref, flow_ref, ret_ref,
    p_ref, u_ref, sx, rx, sy, ry, sc, rc, give, take, send_sem, recv_sem, give_sem, take_sem,
):
    me_x, me_y = lax.axis_index("gx"), lax.axis_index("gy")
    _, extent_x, extent_y, extent_z = state_ref.shape
    halfs = extent_y // BS

    def inside(dx, dy):
        there_x, there_y = me_x + dx, me_y + dy
        return (there_x >= 0) & (there_x < span_x) & (there_y >= 0) & (there_y < span_y)

    def device(dx, dy):
        return (lax.rem(me_x + dx + span_x, span_x), lax.rem(me_y + dy + span_y, span_y))

    barrier = pltpu.get_barrier_semaphore()
    for k in range(1, span_x):
        pl.semaphore_signal(
            barrier, inc=1, device_id=(lax.rem(me_x + k, span_x), me_y), device_id_type=MESH
        )
    for dx, dy in FACES:
        if dy != 0:

            @pl.when(inside(dx, dy))
            def _():
                pl.semaphore_signal(barrier, inc=1, device_id=device(dx, dy), device_id_type=MESH)

    u_ref[...] = jnp.zeros_like(u_ref)
    peers = span_x - 1
    for dx, dy in FACES:
        if dy != 0:
            peers = peers + jnp.where(inside(dx, dy), 1, 0)
    pl.semaphore_wait(barrier, peers)

    omega, omega_first, filled = par_ref[0], par_ref[1], par_ref[2]
    inflow = [par_ref[3], par_ref[4], par_ref[5]]
    inflow_square = inflow[0] * inflow[0] + inflow[1] * inflow[1] + inflow[2] * inflow[2]
    ghost = []
    for c in LATTICE:
        project = c[0] * inflow[0] + c[1] * inflow[1] + c[2] * inflow[2]
        ghost.append(1.0 + 3.0 * project + 4.5 * project * project - 1.5 * inflow_square)

    def buffers(turn, face):
        dx, dy = FACES[face]
        if dy == 0:
            return sx.at[turn, face], rx.at[turn, face]
        if dx == 0:
            return sy.at[turn, face - 2], ry.at[turn, face - 2]
        return sc.at[turn, face - 4], rc.at[turn, face - 4]

    def copy_of(turn, face):
        dx, dy = FACES[face]
        src, dst = buffers(turn, face)
        return pltpu.make_async_remote_copy(
            src_ref=src,
            dst_ref=dst,
            send_sem=send_sem.at[turn, face],
            recv_sem=recv_sem.at[turn, face],
            device_id=device(dx, dy),
            device_id_type=MESH,
        )

    def store(turn, x, h, post):
        for q in range(Q):
            p_ref[turn, q, x + 1, PAD + h * BS : PAD + (h + 1) * BS, :] = post[q]
        if h == halfs - 1:
            for k, q in enumerate(columns_along(0, 1)):
                sy[turn, 0, k, pl.ds(x, 1), :] = post[q][BS - 1 : BS]
        if h == 0:
            for k, q in enumerate(columns_along(0, -1)):
                sy[turn, 1, k, pl.ds(x, 1), :] = post[q][0:1]

    def exchange(turn):
        for face, (dx, dy) in enumerate(FACES):
            x = extent_x if dx > 0 else 1
            y = PAD + extent_y - 1 if dy > 0 else PAD
            if dy == 0:
                for k, q in enumerate(columns_along(dx, dy)):
                    sx[turn, face, k] = p_ref[turn, q, x, PAD : PAD + extent_y, :]
            elif dx != 0:
                (q,) = columns_along(dx, dy)
                sc[turn, face - 4] = p_ref[turn, q, x, y : y + 1, :]

            @pl.when(inside(dx, dy))
            def _():
                copy_of(turn, face).start()

        for face, (dx, dy) in enumerate(FACES):
            x = 0 if dx > 0 else extent_x + 1
            y = PAD - 1 if dy > 0 else PAD + extent_y
            columns = columns_along(dx, dy)

            @pl.when(inside(-dx, -dy))
            def _():
                copy_of(turn, face).wait_recv()
                if dy == 0:
                    for k, q in enumerate(columns):
                        p_ref[turn, q, x, PAD : PAD + extent_y, :] = rx[turn, face, k]
                elif dx == 0:
                    for k, q in enumerate(columns):
                        for i in range(extent_x):
                            p_ref[turn, q, i + 1, y : y + 1, :] = ry[turn, face - 2, k, i : i + 1, :]
                else:
                    p_ref[turn, columns[0], x, y : y + 1, :] = rc[turn, face - 4]

            @pl.when(jnp.logical_not(inside(-dx, -dy)))
            def _():
                for q in columns:
                    if dy == 0:
                        p_ref[turn, q, x, PAD : PAD + extent_y, :] = jnp.full(
                            (extent_y, extent_z), ghost[q]
                        )
                    elif dx == 0:
                        for i in range(extent_x):
                            p_ref[turn, q, i + 1, y : y + 1, :] = jnp.full((1, extent_z), ghost[q])
                    else:
                        p_ref[turn, q, x, y : y + 1, :] = jnp.full((1, extent_z), ghost[q])

    def pulled(turn, x, h):
        g = []
        for q, (cx, cy, cz) in enumerate(LATTICE):
            start = PAD + h * BS - cy
            row = p_ref[turn, q, x + 1 - cx, start : start + BS, :]
            if cz != 0:
                row = pltpu.roll(row, cz % extent_z, 1)
            g.append(row)
        return g

    def push_at(x, h):
        return [field_ref[d, x, h * BS : (h + 1) * BS, :] for d in range(3)]

    fresh = jnp.full((BS, extent_z), filled) > 0.5

    def first(x, carry):
        for h in range(halfs):
            rows = slice(h * BS, (h + 1) * BS)
            g = [state_ref[q, x, rows, :] for q in range(Q)]
            density, velocity = moments(g)
            coarse = [up_ref[d, x // 2, rows, :] for d in range(4)]
            density = jnp.where(fresh, 1.0 + 0.1 * coarse[0], density)
            velocity = [
                jnp.where(fresh, 0.05 * coarse[d + 1], velocity[d]) for d in range(3)
            ]
            store(0, x, h, collide(g, density, velocity, push_at(x, h), omega_first))
        return carry

    lax.fori_loop(0, extent_x, first, 0)
    exchange(0)

    def second(x, carry):
        for h in range(halfs):
            g = pulled(0, x, h)
            density, velocity = moments(g)
            store(1, x, h, collide(g, density, velocity, push_at(x, h), omega))
        return carry

    lax.fori_loop(0, extent_x, second, 0)
    exchange(1)

    for bx in range(extent_x // BS):

        def third(i, carry):
            x = bx * BS + i
            for h in range(halfs):
                g = pulled(1, x, h)
                for q in range(Q):
                    flow_ref[q, x, h * BS : (h + 1) * BS, :] = g[q]
                _, velocity = moments(g)
                c = bx * halfs + h
                for d in range(3):
                    u_ref[
                        pl.ds(pl.multiple_of(d * BS * BS + i * BS, BS), BS),
                        c * extent_z : (c + 1) * extent_z,
                    ] = velocity[d]
            return carry

        lax.fori_loop(0, BS, third, 0)

    high, low = halves(u_ref[...])
    hit = hit_ref[...]
    give[...] = rows_dot(hit, high) + rows_dot(hit, low)
    share = give.shape[0] // span_x

    def give_copy(k):
        there = lax.rem(me_x + k, span_x)
        return pltpu.make_async_remote_copy(
            src_ref=give.at[pl.ds(pl.multiple_of(there * share, BS), share)],
            dst_ref=take.at[pl.ds(pl.multiple_of(me_x * share, BS), share)],
            send_sem=give_sem.at[k],
            recv_sem=take_sem.at[k],
            device_id=(there, me_y),
            device_id_type=MESH,
        )

    def take_copy(k):
        there = lax.rem(me_x + span_x - k, span_x)
        return pltpu.make_async_remote_copy(
            src_ref=give.at[pl.ds(pl.multiple_of(there * share, BS), share)],
            dst_ref=take.at[pl.ds(pl.multiple_of(there * share, BS), share)],
            send_sem=give_sem.at[k],
            recv_sem=take_sem.at[k],
            device_id=(there, me_y),
            device_id_type=MESH,
        )

    for k in range(1, span_x):
        give_copy(k).start()
    own = pl.ds(pl.multiple_of(me_x * share, BS), share)
    take[own, :] = give[own, :]
    for turn in range(2):
        for face, (dx, dy) in enumerate(FACES):

            @pl.when(inside(dx, dy))
            def _():
                copy_of(turn, face).wait_send()

    for k in range(1, span_x):
        give_copy(k).wait_send()
        take_copy(k).wait_recv()
    ret_ref[...] = take[...]


def sample_kernel(ret_ref, slot_ref, pos_ref, out_ref):
    def one(c, carry):
        wx, wy, wz = hats(pos_ref, c)
        slot = slot_ref[c]
        block = ret_ref[pl.ds(pl.multiple_of(slot * BS, BS), BS), :]
        high = block.astype(jnp.bfloat16).astype(jnp.float32)
        left = jnp.concatenate([high, high, block - high], axis=0).T.astype(jnp.bfloat16)
        near = wz.astype(jnp.bfloat16).astype(jnp.float32)
        right = jnp.concatenate([near, wz - near, near], axis=0).astype(jnp.bfloat16)
        lines = plain_dot(left, right)
        for d in range(3):
            total = None
            for x in range(BS):
                start = (d * BS + x) * BS
                term = wx[x : x + 1] * lines[start : start + BS]
                total = term if total is None else total + term
            out_ref[d, pl.ds(c, 1), :] = VELOCITY_UNIT * jnp.sum(total * wy, axis=0, keepdims=True)
        return carry

    lax.fori_loop(0, pos_ref.shape[1], one, 0)


VMEM = pl.BlockSpec(memory_space=pltpu.VMEM)
SMEM = pl.BlockSpec(memory_space=pltpu.SMEM)


def body(
    populations,
    coarse_state,
    window_shift,
    inflow,
    relaxation,
    positions,
    rest_shape,
    stiffness,
    cell_owner,
    cell_block,
    triangles,
):
    span_x = lax.axis_size("gx")
    span_y = lax.axis_size("gy")
    here_x = lax.axis_index("gx")
    _, extent_x, extent_y, extent_z = populations.shape
    cells, _, count = positions.shape
    positions = positions.transpose(1, 0, 2)
    cap = 2 * cells // span_x
    slots = span_x * cap
    width = 256
    blocks = extent_x // BS * (extent_y // BS) * (extent_z // BS)
    f32 = jnp.float32
    shift = window_shift[0]

    def cell_part(positions, rest_shape, stiffness, owner, block, triangles, coarse):
        outgoing, slot = pl.pallas_call(
            functools.partial(spread_kernel, span_x, cap),
            out_shape=(
                jax.ShapeDtypeStruct((slots * BS, width), f32),
                jax.ShapeDtypeStruct((cells,), jnp.int32),
            ),
            in_specs=[VMEM, VMEM, SMEM, SMEM, SMEM, VMEM],
            out_specs=(VMEM, SMEM),
            scratch_shapes=[
                pltpu.VMEM((3, cells, count), f32),
                pltpu.SMEM((span_x,), jnp.int32),
            ],
            compiler_params=pltpu.CompilerParams(vmem_limit_bytes=48 << 20),
            cost_estimate=pl.CostEstimate(
                flops=2_000_000_000, bytes_accessed=4_000_000, transcendentals=0
            ),
            name="spread",
        )(positions, rest_shape, stiffness, owner, block, triangles)
        arrived = lax.all_to_all(outgoing, "gx", split_axis=0, concat_axis=0, tiled=True)
        field, up, hit = pl.pallas_call(
            field_kernel,
            out_shape=(
                jax.ShapeDtypeStruct((3, extent_x, extent_y, extent_z), f32),
                jax.ShapeDtypeStruct((4, extent_x // 2, extent_y, extent_z), f32),
                jax.ShapeDtypeStruct((slots * BS, blocks * BS), jnp.bfloat16),
            ),
            in_specs=[VMEM, VMEM],
            out_specs=(VMEM, VMEM, VMEM),
            compiler_params=pltpu.CompilerParams(vmem_limit_bytes=48 << 20),
            cost_estimate=pl.CostEstimate(
                flops=500_000_000, bytes_accessed=3_000_000, transcendentals=0
            ),
            name="field",
        )(arrived, coarse)
        return slot, field, up, hit

    def moved_by(distance, populations, *rest):
        pairs = [(i, i - distance) for i in range(distance, span_x)]
        moved = lax.ppermute(populations, "gx", pairs)
        return (moved,) + cell_part(*rest)

    coarse = coarse_state.reshape(-1, coarse_state.shape[3])
    moved, slot, field, up, hit = lax.switch(
        shift - 1,
        [functools.partial(moved_by, distance) for distance in range(1, span_x)],
        populations,
        positions,
        rest_shape,
        stiffness,
        cell_owner[:, 0],
        cell_block,
        triangles,
        coarse,
    )
    entering = here_x + shift >= span_x
    omega = relaxation[0]
    par = jnp.concatenate(
        [
            jnp.stack([omega, jnp.where(entering, 1.0, omega), jnp.where(entering, 1.0, 0.0)]),
            inflow,
        ]
    )
    faces = len(FACES)
    flow, ret = pl.pallas_call(
        functools.partial(flow_kernel, span_x, span_y),
        out_shape=(
            jax.ShapeDtypeStruct(populations.shape, f32),
            jax.ShapeDtypeStruct((slots * BS, width), f32),
        ),
        in_specs=[VMEM, VMEM, VMEM, VMEM, SMEM],
        out_specs=(VMEM, VMEM),
        scratch_shapes=[
            pltpu.VMEM((2, Q, extent_x + 2, extent_y + 2 * PAD, extent_z), f32),
            pltpu.VMEM((width, blocks * BS), f32),
            pltpu.VMEM((2, 2, 5, extent_y, extent_z), f32),
            pltpu.VMEM((2, 2, 5, extent_y, extent_z), f32),
            pltpu.VMEM((2, 2, 5, extent_x, extent_z), f32),
            pltpu.VMEM((2, 2, 5, extent_x, extent_z), f32),
            pltpu.VMEM((2, 4, 1, extent_z), f32),
            pltpu.VMEM((2, 4, 1, extent_z), f32),
            pltpu.VMEM((slots * BS, width), f32),
            pltpu.VMEM((slots * BS, width), f32),
            pltpu.SemaphoreType.DMA((2, faces)),
            pltpu.SemaphoreType.DMA((2, faces)),
            pltpu.SemaphoreType.DMA((span_x,)),
            pltpu.SemaphoreType.DMA((span_x,)),
        ],
        compiler_params=pltpu.CompilerParams(
            collective_id=0, has_side_effects=True, vmem_limit_bytes=48 << 20
        ),
        cost_estimate=pl.CostEstimate(
            flops=100_000_000, bytes_accessed=8_000_000, transcendentals=0
        ),
        name="flow",
    )(moved, field, up, hit, par)
    cell_velocity = pl.pallas_call(
        sample_kernel,
        out_shape=jax.ShapeDtypeStruct(positions.shape, f32),
        in_specs=[VMEM, SMEM, VMEM],
        out_specs=VMEM,
        compiler_params=pltpu.CompilerParams(vmem_limit_bytes=48 << 20),
        cost_estimate=pl.CostEstimate(
            flops=200_000_000, bytes_accessed=1_000_000, transcendentals=0
        ),
        name="sample",
    )(ret, slot, positions)
    return (flow, cell_velocity.transpose(1, 0, 2))


def solution(mesh):
    placed = (
        P(None, "gx", "gy", None),
        P(None, "gx", "gy", None),
        P(),
        P(),
        P(),
        P(("gx", "gy"), None, None),
        P(),
        P(("gx", "gy")),
        P(("gx", "gy"), None),
        P(("gx", "gy")),
        P(),
    )
    return jax.shard_map(
        body,
        mesh=mesh,
        in_specs=placed,
        out_specs=(P(None, "gx", "gy", None), P(("gx", "gy"), None, None)),
        check_vma=False,
    )
```

```python
import functools
import jax
import jax.numpy as jnp
from jax import lax
from jax.experimental import pallas as pl
from jax.experimental.pallas import tpu as pltpu
from jax.sharding import PartitionSpec as P

BS = 8
LATTICE = (
    (0, 0, 0),
    (1, 0, 0),
    (-1, 0, 0),
    (0, 1, 0),
    (0, -1, 0),
    (0, 0, 1),
    (0, 0, -1),
    (1, 1, 0),
    (-1, -1, 0),
    (1, -1, 0),
    (-1, 1, 0),
    (1, 0, 1),
    (-1, 0, -1),
    (1, 0, -1),
    (-1, 0, 1),
    (0, 1, 1),
    (0, -1, -1),
    (0, 1, -1),
    (0, -1, 1),
)
Q = len(LATTICE)
COUPLING = 0.001
VELOCITY_UNIT = 20.0
HIGHEST = lax.Precision.HIGHEST
MESH = pl.DeviceIdType.MESH
PAD = 8
FACES = ((1, 0), (-1, 0), (0, 1), (0, -1), (1, 1), (-1, -1), (1, -1), (-1, 1))


def columns_along(dx, dy):
    return [
        q
        for q, (cx, cy, _) in enumerate(LATTICE)
        if (dx == 0 or cx == dx) and (dy == 0 or cy == dy)
    ]


def halves(x):
    high = x.astype(jnp.bfloat16)
    low = (x - high.astype(jnp.float32)).astype(jnp.bfloat16)
    return high, low


def rows_dot(a, b):
    return lax.dot_general(a, b, (((1,), (1,)), ((), ())), preferred_element_type=jnp.float32)


def plain_dot(a, b):
    return lax.dot_general(a, b, (((1,), (0,)), ((), ())), preferred_element_type=jnp.float32)


def grouped(number, one):
    size = 4 if number % 4 == 0 else 1

    def group(i, carry):
        for j in range(size):
            one(i * size + j)
        return carry

    lax.fori_loop(0, number // size, group, 0)


def hats(pos_ref, c):
    nodes = lax.broadcasted_iota(jnp.int32, (BS, pos_ref.shape[2]), 0).astype(jnp.float32)
    return [
        jnp.maximum(0.0, 1.0 - jnp.abs(pos_ref[d, pl.ds(c, 1), :] - nodes)) for d in range(3)
    ]


def spread_kernel(
    span, cap, pos_ref, rest_ref, stiff_ref, owner_ref, block_ref, tri_ref, coarse_ref,
    out_ref, slot_ref, up_ref, force_ref, count_ref,
):
    _, cells, count = pos_ref.shape
    tri = tri_ref[...]
    vertices = lax.broadcasted_iota(jnp.int32, (tri.shape[0], count), 1)
    hit = (tri[:, 0:1] == vertices) | (tri[:, 1:2] == vertices) | (tri[:, 2:3] == vertices)
    member = jnp.where(hit, 1.0, 0.0)
    degree = jnp.sum(member, axis=0, keepdims=True)
    member = member.astype(jnp.bfloat16)
    gap = jnp.concatenate([pos_ref[d] - rest_ref[d : d + 1, :] for d in range(3)], axis=0)
    high, low = halves(gap)
    each = rows_dot(high, member) + rows_dot(low, member)
    high, low = halves(each)
    back = plain_dot(high, member) + plain_dot(low, member)
    force_ref[...] = (back - 3.0 * degree * gap).reshape(3, cells, count)
    coarse = coarse_ref[...]
    rows, depth = coarse.shape
    extent_z = up_ref.shape[3]
    pick_z = jnp.where(
        lax.broadcasted_iota(jnp.int32, (depth, extent_z), 1) // 2
        == lax.broadcasted_iota(jnp.int32, (depth, extent_z), 0),
        1.0,
        0.0,
    )
    pick_y = jnp.where(
        lax.broadcasted_iota(jnp.int32, (2 * rows, rows), 0) // 2
        == lax.broadcasted_iota(jnp.int32, (2 * rows, rows), 1),
        1.0,
        0.0,
    )
    along = jnp.dot(coarse, pick_z, precision=HIGHEST, preferred_element_type=jnp.float32)
    wide = jnp.dot(pick_y, along, precision=HIGHEST, preferred_element_type=jnp.float32)
    up_ref[...] = wide.reshape(up_ref.shape)
    out_ref[...] = jnp.zeros_like(out_ref)
    for o in range(span):
        count_ref[o] = 0
    lanes = lax.broadcasted_iota(jnp.int32, (BS, out_ref.shape[1]), 1)
    used = 3 * BS * BS
    spare = jnp.zeros((out_ref.shape[1] - used, count), jnp.bfloat16)

    def one(c):
        wx, wy, wz = hats(pos_ref, c)
        rows = []
        for d in range(3):
            push = force_ref[d, pl.ds(c, 1), :] * stiff_ref[c]
            for x in range(BS):
                rows.append((push * wx[x : x + 1]) * wy)
        high, low = halves(jnp.concatenate(rows, axis=0))
        weights = jnp.concatenate(halves(wz), axis=0)
        first = rows_dot(weights, jnp.concatenate([high, spare], axis=0))
        second = rows_dot(weights, jnp.concatenate([low, spare], axis=0))
        block = first[:BS] + first[BS:] + second[:BS]
        tag = (block_ref[c] + 1).astype(jnp.float32)
        owner = owner_ref[c]
        rank = count_ref[owner]
        count_ref[owner] = rank + 1
        slot = owner * cap + rank
        slot_ref[c] = slot
        out_ref[pl.ds(pl.multiple_of(slot * BS, BS), BS), :] = jnp.where(lanes < used, block, tag)

    grouped(cells, one)


def place_forces(arrived_ref, field_ref, hit_ref):
    _, extent_x, extent_y, extent_z = field_ref.shape
    used = 3 * BS * BS
    slots, width = hit_ref.shape
    tag = arrived_ref[:, used : used + 1]
    row = lax.broadcasted_iota(jnp.int32, (slots, width), 0)
    col = lax.broadcasted_iota(jnp.int32, (slots, width), 1)
    same = (tag - 1.0 == (col // BS).astype(jnp.float32)) & (row % BS == col % BS)
    hit = jnp.where(same, 1.0, 0.0).astype(jnp.bfloat16)
    hit_ref[...] = hit
    high, low = halves(arrived_ref[...].T)
    placed = COUPLING * (plain_dot(high, hit) + plain_dot(low, hit))
    across = extent_y // BS
    for bx in range(extent_x // BS):
        for by in range(across):
            c = bx * across + by
            for d in range(3):
                part = placed[d * BS * BS : (d + 1) * BS * BS, c * extent_z : (c + 1) * extent_z]
                field_ref[d, bx * BS : (bx + 1) * BS, by * BS : (by + 1) * BS, :] = part.reshape(
                    BS, BS, extent_z
                )


def moments(g):
    axis_sum = (g[1] + g[2]) + (g[3] + g[4]) + (g[5] + g[6])
    edge_sum = g[7]
    for q in range(8, Q):
        edge_sum = edge_sum + g[q]
    density = g[0] * (1.0 / 3.0) + axis_sum * (1.0 / 18.0) + edge_sum * (1.0 / 36.0)
    pair = {q: g[q] - g[q + 1] for q in range(1, Q, 2)}
    inverse = 1.0 / density
    velocity = []
    for d in range(3):
        axis, edge = None, None
        for q in range(1, Q, 2):
            sign = LATTICE[q][d]
            if sign == 0:
                continue
            term = pair[q] if sign > 0 else -pair[q]
            if q < 7:
                axis = term
            else:
                edge = term if edge is None else edge + term
        velocity.append((axis * (1.0 / 18.0) + edge * (1.0 / 36.0)) * inverse)
    return density, velocity


def along(c, v):
    total = None
    for d in range(3):
        if c[d] != 0:
            term = v[d] if c[d] > 0 else -v[d]
            total = term if total is None else total + term
    return total


def collide(g, density, velocity, force, omega):
    square = velocity[0] * velocity[0] + velocity[1] * velocity[1] + velocity[2] * velocity[2]
    base = 1.0 - 1.5 * square
    rated = omega * density
    keep = 1.0 - omega
    post = [keep * g[0] + rated * base]
    for q in range(1, Q, 2):
        project = along(LATTICE[q], velocity)
        even = rated * (base + 4.5 * (project * project))
        odd = 3.0 * (rated * project + along(LATTICE[q], force))
        post.append(keep * g[q] + (even + odd))
        post.append(keep * g[q + 1] + (even - odd))
    return post


def flow_kernel(
    span_x, span_y, state_ref, cut_refs, outgoing_ref, up_ref, par_ref, flow_ref, ret_ref,
    arrived, field_ref, hit_ref, p_ref, u_ref, sx, rx, sy, ry, sc, rc, give, take, send_sem, recv_sem, give_sem, take_sem, go_sem, come_sem,
):
    me_x, me_y = lax.axis_index("gx"), lax.axis_index("gy")
    _, extent_x, extent_y, extent_z = state_ref.shape
    halfs = extent_y // BS

    def inside(dx, dy):
        there_x, there_y = me_x + dx, me_y + dy
        return (there_x >= 0) & (there_x < span_x) & (there_y >= 0) & (there_y < span_y)

    def device(dx, dy):
        return (lax.rem(me_x + dx + span_x, span_x), lax.rem(me_y + dy + span_y, span_y))

    barrier = pltpu.get_barrier_semaphore()
    for k in range(1, span_x):
        pl.semaphore_signal(
            barrier, inc=1, device_id=(lax.rem(me_x + k, span_x), me_y), device_id_type=MESH
        )
    for dx, dy in FACES:
        if dy != 0:

            @pl.when(inside(dx, dy))
            def _():
                pl.semaphore_signal(barrier, inc=1, device_id=device(dx, dy), device_id_type=MESH)

    share = give.shape[0] // span_x

    def part(index):
        return pl.ds(pl.multiple_of(index * share, BS), share)

    own = part(me_x)

    def copy_out(src, dst, out_sem, in_sem, k):
        there = lax.rem(me_x + k, span_x)
        return pltpu.make_async_remote_copy(
            src_ref=src.at[part(there)],
            dst_ref=dst.at[own],
            send_sem=out_sem.at[k],
            recv_sem=in_sem.at[k],
            device_id=(there, me_y),
            device_id_type=MESH,
        )

    def copy_in(src, dst, out_sem, in_sem, k):
        there = lax.rem(me_x + span_x - k, span_x)
        return pltpu.make_async_remote_copy(
            src_ref=src.at[part(there)],
            dst_ref=dst.at[part(there)],
            send_sem=out_sem.at[k],
            recv_sem=in_sem.at[k],
            device_id=(there, me_y),
            device_id_type=MESH,
        )

    u_ref[...] = jnp.zeros_like(u_ref)
    peers = span_x - 1
    for dx, dy in FACES:
        if dy != 0:
            peers = peers + jnp.where(inside(dx, dy), 1, 0)
    pl.semaphore_wait(barrier, peers)
    for k in range(1, span_x):
        copy_out(outgoing_ref, arrived, go_sem, come_sem, k).start()
    arrived[own, :] = outgoing_ref[own, :]

    omega, omega_first, filled = par_ref[0], par_ref[1], par_ref[2]
    inflow = [par_ref[3], par_ref[4], par_ref[5]]
    inflow_square = inflow[0] * inflow[0] + inflow[1] * inflow[1] + inflow[2] * inflow[2]
    ghost = []
    for c in LATTICE:
        project = c[0] * inflow[0] + c[1] * inflow[1] + c[2] * inflow[2]
        ghost.append(1.0 + 3.0 * project + 4.5 * project * project - 1.5 * inflow_square)

    def buffers(turn, face):
        dx, dy = FACES[face]
        if dy == 0:
            return sx.at[turn, face], rx.at[turn, face]
        if dx == 0:
            return sy.at[turn, face - 2], ry.at[turn, face - 2]
        return sc.at[turn, face - 4], rc.at[turn, face - 4]

    def copy_of(turn, face):
        dx, dy = FACES[face]
        src, dst = buffers(turn, face)
        return pltpu.make_async_remote_copy(
            src_ref=src,
            dst_ref=dst,
            send_sem=send_sem.at[turn, face],
            recv_sem=recv_sem.at[turn, face],
            device_id=device(dx, dy),
            device_id_type=MESH,
        )

    def store(turn, x, h, post):
        for q in range(Q):
            p_ref[turn, q, x + 1, PAD + h * BS : PAD + (h + 1) * BS, :] = post[q]
        if h == halfs - 1:
            for k, q in enumerate(columns_along(0, 1)):
                sy[turn, 0, k, pl.ds(x, 1), :] = post[q][BS - 1 : BS]
        if h == 0:
            for k, q in enumerate(columns_along(0, -1)):
                sy[turn, 1, k, pl.ds(x, 1), :] = post[q][0:1]

    def exchange(turn):
        for face, (dx, dy) in enumerate(FACES):
            x = extent_x if dx > 0 else 1
            y = PAD + extent_y - 1 if dy > 0 else PAD
            if dy == 0:
                for k, q in enumerate(columns_along(dx, dy)):
                    sx[turn, face, k] = p_ref[turn, q, x, PAD : PAD + extent_y, :]
            elif dx != 0:
                (q,) = columns_along(dx, dy)
                sc[turn, face - 4] = p_ref[turn, q, x, y : y + 1, :]

            @pl.when(inside(dx, dy))
            def _():
                copy_of(turn, face).start()

        for face, (dx, dy) in enumerate(FACES):
            x = 0 if dx > 0 else extent_x + 1
            y = PAD - 1 if dy > 0 else PAD + extent_y
            columns = columns_along(dx, dy)

            @pl.when(inside(-dx, -dy))
            def _():
                copy_of(turn, face).wait_recv()
                if dy == 0:
                    for k, q in enumerate(columns):
                        p_ref[turn, q, x, PAD : PAD + extent_y, :] = rx[turn, face, k]
                elif dx == 0:
                    for k, q in enumerate(columns):
                        for i in range(extent_x):
                            p_ref[turn, q, i + 1, y : y + 1, :] = ry[turn, face - 2, k, i : i + 1, :]
                else:
                    p_ref[turn, columns[0], x, y : y + 1, :] = rc[turn, face - 4]

            @pl.when(jnp.logical_not(inside(-dx, -dy)))
            def _():
                for q in columns:
                    if dy == 0:
                        p_ref[turn, q, x, PAD : PAD + extent_y, :] = jnp.full(
                            (extent_y, extent_z), ghost[q]
                        )
                    elif dx == 0:
                        for i in range(extent_x):
                            p_ref[turn, q, i + 1, y : y + 1, :] = jnp.full((1, extent_z), ghost[q])
                    else:
                        p_ref[turn, q, x, y : y + 1, :] = jnp.full((1, extent_z), ghost[q])

    def pulled(turn, x, h):
        g = []
        for q, (cx, cy, cz) in enumerate(LATTICE):
            start = PAD + h * BS - cy
            row = p_ref[turn, q, x + 1 - cx, start : start + BS, :]
            if cz != 0:
                row = pltpu.roll(row, cz % extent_z, 1)
            g.append(row)
        return g

    def push_at(x, h):
        return [field_ref[d, x, h * BS : (h + 1) * BS, :] for d in range(3)]

    for k in range(1, span_x):
        copy_in(outgoing_ref, arrived, go_sem, come_sem, k).wait_recv()
    place_forces(arrived, field_ref, hit_ref)
    starts = [0]
    for cut_ref in cut_refs:
        starts.append(starts[-1] + cut_ref.shape[0])
    fresh = jnp.full((BS, extent_z), filled) > 0.5

    def first(x, carry):
        for h in range(halfs):
            rows = slice(h * BS, (h + 1) * BS)
            g = []
            for cut_ref, begin, end in zip(cut_refs, starts, starts[1:]):
                for q in range(begin, end):
                    g.append(state_ref[q, x, rows, :] + cut_ref[q - begin, x, rows, :])
            density, velocity = moments(g)
            coarse = [up_ref[d, x // 2, rows, :] for d in range(4)]
            density = jnp.where(fresh, 1.0 + 0.1 * coarse[0], density)
            velocity = [
                jnp.where(fresh, 0.05 * coarse[d + 1], velocity[d]) for d in range(3)
            ]
            store(0, x, h, collide(g, density, velocity, push_at(x, h), omega_first))
        return carry

    lax.fori_loop(0, extent_x, first, 0)
    exchange(0)

    def second(x, carry):
        for h in range(halfs):
            g = pulled(0, x, h)
            density, velocity = moments(g)
            store(1, x, h, collide(g, density, velocity, push_at(x, h), omega))
        return carry

    lax.fori_loop(0, extent_x, second, 0)
    exchange(1)

    for bx in range(extent_x // BS):

        def third(i, carry):
            x = bx * BS + i
            for h in range(halfs):
                g = pulled(1, x, h)
                for q in range(Q):
                    flow_ref[q, x, h * BS : (h + 1) * BS, :] = g[q]
                _, velocity = moments(g)
                c = bx * halfs + h
                for d in range(3):
                    u_ref[
                        pl.ds(pl.multiple_of(d * BS * BS + i * BS, BS), BS),
                        c * extent_z : (c + 1) * extent_z,
                    ] = velocity[d]
            return carry

        lax.fori_loop(0, BS, third, 0)

    high, low = halves(u_ref[...])
    hit = hit_ref[...]
    give[...] = rows_dot(hit, high) + rows_dot(hit, low)

    for k in range(1, span_x):
        copy_out(give, take, give_sem, take_sem, k).start()
    take[own, :] = give[own, :]
    for turn in range(2):
        for face, (dx, dy) in enumerate(FACES):

            @pl.when(inside(dx, dy))
            def _():
                copy_of(turn, face).wait_send()

    for k in range(1, span_x):
        copy_out(give, take, give_sem, take_sem, k).wait_send()
        copy_in(give, take, give_sem, take_sem, k).wait_recv()
        copy_out(outgoing_ref, arrived, go_sem, come_sem, k).wait_send()
    ret_ref[...] = take[...]


def sample_kernel(ret_ref, slot_ref, pos_ref, out_ref):
    def one(c):
        wx, wy, wz = hats(pos_ref, c)
        slot = slot_ref[c]
        block = ret_ref[pl.ds(pl.multiple_of(slot * BS, BS), BS), :]
        high = block.astype(jnp.bfloat16).astype(jnp.float32)
        left = jnp.concatenate([high, high, block - high], axis=0).T.astype(jnp.bfloat16)
        near = wz.astype(jnp.bfloat16).astype(jnp.float32)
        right = jnp.concatenate([near, wz - near, near], axis=0).astype(jnp.bfloat16)
        lines = plain_dot(left[: 3 * BS * BS], right)
        for d in range(3):
            total = None
            for x in range(BS):
                start = (d * BS + x) * BS
                term = wx[x : x + 1] * lines[start : start + BS]
                total = term if total is None else total + term
            out_ref[d, pl.ds(c, 1), :] = VELOCITY_UNIT * jnp.sum(total * wy, axis=0, keepdims=True)

    grouped(pos_ref.shape[1], one)


VMEM = pl.BlockSpec(memory_space=pltpu.VMEM)
SMEM = pl.BlockSpec(memory_space=pltpu.SMEM)


CUTS = (0, 10, 13, 19)


def routes_of(mesh):
    line = list(mesh.devices[:, 0])
    span = len(line)
    places = []
    for device in line:
        coords = getattr(device, "coords", None)
        if coords is None:
            return {s: ([(i, i - s) for i in range(s, span)], [], [], [], (0, 0, 0)) for s in range(1, span)}
        places.append((coords[0], coords[1], getattr(device, "core_on_chip", 0)))
    routes = {}
    for s in range(1, span):
        pairs = [(i, i - s) for i in range(s, span)]
        turning, hop, onward = [], [], []
        for i, j in pairs:
            corner = (places[i][0], places[j][1], places[j][2])
            if places[i][0] != places[j][0] and places[i][1] != places[j][1] and corner in places:
                relay = places.index(corner)
                turning.append((i, j))
                hop.append((i, relay))
                onward.append((relay, j))
        plain = [pair for pair in pairs if pair not in turning]
        load = {}
        for i, j in plain:
            leg = places[i][:2] + places[j][:2]
            load[leg] = load.get(leg, 0) + 1
        crowded = any(places[i][:2] + places[j][:2] in load for i, j in hop)
        relays = [j for _, j in hop]
        idle = not turning or (plain and not crowded)
        if len(set(relays)) < len(relays) or max(load.values(), default=0) > 1 or idle:
            routes[s] = (pairs, [], [], [], (0, 0, 0))
        elif crowded:
            routes[s] = (plain, turning, hop, onward, (0, 1, 1))
        else:
            routes[s] = (plain, turning, hop, onward, (0, 0, 1))
    return routes


def body(
    routes,
    populations,
    coarse_state,
    window_shift,
    inflow,
    relaxation,
    positions,
    rest_shape,
    stiffness,
    cell_owner,
    cell_block,
    triangles,
):
    span_x = lax.axis_size("gx")
    span_y = lax.axis_size("gy")
    here_x = lax.axis_index("gx")
    _, extent_x, extent_y, extent_z = populations.shape
    cells, _, count = positions.shape
    positions = positions.transpose(1, 0, 2)
    cap = 2 * cells // span_x
    slots = span_x * cap
    width = 256
    blocks = extent_x // BS * (extent_y // BS) * (extent_z // BS)
    f32 = jnp.float32
    shift = window_shift[0]

    def cell_part(positions, rest_shape, stiffness, owner, block, triangles, coarse):
        return pl.pallas_call(
            functools.partial(spread_kernel, span_x, cap),
            out_shape=(
                jax.ShapeDtypeStruct((slots * BS, width), f32),
                jax.ShapeDtypeStruct((cells,), jnp.int32),
                jax.ShapeDtypeStruct((4, extent_x // 2, extent_y, extent_z), f32),
            ),
            in_specs=[VMEM, VMEM, SMEM, SMEM, SMEM, VMEM, VMEM],
            out_specs=(VMEM, SMEM, VMEM),
            scratch_shapes=[
                pltpu.VMEM((3, cells, count), f32),
                pltpu.SMEM((span_x,), jnp.int32),
            ],
            compiler_params=pltpu.CompilerParams(vmem_limit_bytes=48 << 20),
            cost_estimate=pl.CostEstimate(
                flops=2_000_000_000, bytes_accessed=4_000_000, transcendentals=0
            ),
            name="spread",
        )(positions, rest_shape, stiffness, owner, block, triangles, coarse)

    def moved_by(distance, populations, *rest):
        plain, turning, hop, onward, ways = routes[distance]
        whole = lax.ppermute(populations, "gx", plain) if plain else jnp.zeros_like(populations)
        outgoing, slot, up = cell_part(*rest)
        cuts = []
        for begin, end, way in zip(CUTS, CUTS[1:], ways):
            cut = populations[begin:end]
            if not turning:
                cut = jnp.zeros_like(cut)
            elif way:
                cut, outgoing = lax.optimization_barrier((lax.ppermute(cut, "gx", hop), outgoing))
                cut = lax.ppermute(cut, "gx", onward)
            else:
                cut = lax.ppermute(cut, "gx", turning)
            cuts.append(cut)
        return whole, tuple(cuts), outgoing, slot, up

    coarse = coarse_state.reshape(-1, coarse_state.shape[3])
    whole, cuts, outgoing, slot, up = lax.switch(
        shift - 1,
        [functools.partial(moved_by, distance) for distance in range(1, span_x)],
        populations,
        positions,
        rest_shape,
        stiffness,
        cell_owner[:, 0],
        cell_block,
        triangles,
        coarse,
    )
    entering = here_x + shift >= span_x
    omega = relaxation[0]
    par = jnp.concatenate(
        [
            jnp.stack([omega, jnp.where(entering, 1.0, omega), jnp.where(entering, 1.0, 0.0)]),
            inflow,
        ]
    )
    faces = len(FACES)
    flow, ret = pl.pallas_call(
        functools.partial(flow_kernel, span_x, span_y),
        out_shape=(
            jax.ShapeDtypeStruct(populations.shape, f32),
            jax.ShapeDtypeStruct((slots * BS, width), f32),
        ),
        in_specs=[VMEM, [VMEM] * len(cuts), VMEM, VMEM, SMEM],
        out_specs=(VMEM, VMEM),
        scratch_shapes=[
            pltpu.VMEM((slots * BS, width), f32),
            pltpu.VMEM((3, extent_x, extent_y, extent_z), f32),
            pltpu.VMEM((slots * BS, blocks * BS), jnp.bfloat16),
            pltpu.VMEM((2, Q, extent_x + 2, extent_y + 2 * PAD, extent_z), f32),
            pltpu.VMEM((width, blocks * BS), f32),
            pltpu.VMEM((2, 2, 5, extent_y, extent_z), f32),
            pltpu.VMEM((2, 2, 5, extent_y, extent_z), f32),
            pltpu.VMEM((2, 2, 5, extent_x, extent_z), f32),
            pltpu.VMEM((2, 2, 5, extent_x, extent_z), f32),
            pltpu.VMEM((2, 4, 1, extent_z), f32),
            pltpu.VMEM((2, 4, 1, extent_z), f32),
            pltpu.VMEM((slots * BS, width), f32),
            pltpu.VMEM((slots * BS, width), f32),
            pltpu.SemaphoreType.DMA((2, faces)),
            pltpu.SemaphoreType.DMA((2, faces)),
            pltpu.SemaphoreType.DMA((span_x,)),
            pltpu.SemaphoreType.DMA((span_x,)),
            pltpu.SemaphoreType.DMA((span_x,)),
            pltpu.SemaphoreType.DMA((span_x,)),
        ],
        compiler_params=pltpu.CompilerParams(
            collective_id=0, has_side_effects=True, vmem_limit_bytes=48 << 20
        ),
        cost_estimate=pl.CostEstimate(
            flops=100_000_000, bytes_accessed=8_000_000, transcendentals=0
        ),
        name="flow",
    )(whole, list(cuts), outgoing, up, par)
    cell_velocity = pl.pallas_call(
        sample_kernel,
        out_shape=jax.ShapeDtypeStruct(positions.shape, f32),
        in_specs=[VMEM, SMEM, VMEM],
        out_specs=VMEM,
        compiler_params=pltpu.CompilerParams(vmem_limit_bytes=48 << 20),
        cost_estimate=pl.CostEstimate(
            flops=200_000_000, bytes_accessed=1_000_000, transcendentals=0
        ),
        name="sample",
    )(ret, slot, positions)
    return (flow, cell_velocity.transpose(1, 0, 2))


def solution(mesh):
    placed = (
        P(None, "gx", "gy", None),
        P(None, "gx", "gy", None),
        P(),
        P(),
        P(),
        P(("gx", "gy"), None, None),
        P(),
        P(("gx", "gy")),
        P(("gx", "gy"), None),
        P(("gx", "gy")),
        P(),
    )
    return jax.shard_map(
        functools.partial(body, routes_of(mesh)),
        mesh=mesh,
        in_specs=placed,
        out_specs=(P(None, "gx", "gy", None), P(("gx", "gy"), None, None)),
        check_vma=False,
    )
```

```python
import functools
import jax
import jax.numpy as jnp
from jax import lax
from jax.experimental import pallas as pl
from jax.experimental.pallas import tpu as pltpu
from jax.sharding import PartitionSpec as P

BS = 8
LATTICE = (
    (0, 0, 0),
    (1, 0, 0),
    (-1, 0, 0),
    (0, 1, 0),
    (0, -1, 0),
    (0, 0, 1),
    (0, 0, -1),
    (1, 1, 0),
    (-1, -1, 0),
    (1, -1, 0),
    (-1, 1, 0),
    (1, 0, 1),
    (-1, 0, -1),
    (1, 0, -1),
    (-1, 0, 1),
    (0, 1, 1),
    (0, -1, -1),
    (0, 1, -1),
    (0, -1, 1),
)
Q = len(LATTICE)
COUPLING = 0.001
VELOCITY_UNIT = 20.0
HIGHEST = lax.Precision.HIGHEST
MESH = pl.DeviceIdType.MESH
PAD = 8
FACES = ((1, 0), (-1, 0), (0, 1), (0, -1), (1, 1), (-1, -1), (1, -1), (-1, 1))


def columns_along(dx, dy):
    return [
        q
        for q, (cx, cy, _) in enumerate(LATTICE)
        if (dx == 0 or cx == dx) and (dy == 0 or cy == dy)
    ]


def halves(x):
    high = x.astype(jnp.bfloat16)
    low = (x - high.astype(jnp.float32)).astype(jnp.bfloat16)
    return high, low


def rows_dot(a, b):
    return lax.dot_general(a, b, (((1,), (1,)), ((), ())), preferred_element_type=jnp.float32)


def plain_dot(a, b):
    return lax.dot_general(a, b, (((1,), (0,)), ((), ())), preferred_element_type=jnp.float32)


def grouped(number, one):
    size = 4 if number % 4 == 0 else 1

    def group(i, carry):
        for j in range(size):
            one(i * size + j)
        return carry

    lax.fori_loop(0, number // size, group, 0)


def hats(pos_ref, c):
    nodes = lax.broadcasted_iota(jnp.int32, (BS, pos_ref.shape[2]), 0).astype(jnp.float32)
    return [
        jnp.maximum(0.0, 1.0 - jnp.abs(pos_ref[d, pl.ds(c, 1), :] - nodes)) for d in range(3)
    ]


def spread_kernel(
    span, cap, pos_ref, rest_ref, stiff_ref, owner_ref, block_ref, tri_ref, coarse_ref,
    out_ref, slot_ref, up_ref, force_ref, count_ref,
):
    _, cells, count = pos_ref.shape
    tri = tri_ref[...]
    vertices = lax.broadcasted_iota(jnp.int32, (tri.shape[0], count), 1)
    hit = (tri[:, 0:1] == vertices) | (tri[:, 1:2] == vertices) | (tri[:, 2:3] == vertices)
    member = jnp.where(hit, 1.0, 0.0)
    degree = jnp.sum(member, axis=0, keepdims=True)
    member = member.astype(jnp.bfloat16)
    gap = jnp.concatenate([pos_ref[d] - rest_ref[d : d + 1, :] for d in range(3)], axis=0)
    high, low = halves(gap)
    each = rows_dot(high, member) + rows_dot(low, member)
    high, low = halves(each)
    back = plain_dot(high, member) + plain_dot(low, member)
    force_ref[...] = (back - 3.0 * degree * gap).reshape(3, cells, count)
    coarse = coarse_ref[...]
    rows, depth = coarse.shape
    extent_z = up_ref.shape[3]
    pick_z = jnp.where(
        lax.broadcasted_iota(jnp.int32, (depth, extent_z), 1) // 2
        == lax.broadcasted_iota(jnp.int32, (depth, extent_z), 0),
        1.0,
        0.0,
    )
    pick_y = jnp.where(
        lax.broadcasted_iota(jnp.int32, (2 * rows, rows), 0) // 2
        == lax.broadcasted_iota(jnp.int32, (2 * rows, rows), 1),
        1.0,
        0.0,
    )
    along = jnp.dot(coarse, pick_z, precision=HIGHEST, preferred_element_type=jnp.float32)
    wide = jnp.dot(pick_y, along, precision=HIGHEST, preferred_element_type=jnp.float32)
    up_ref[...] = wide.reshape(up_ref.shape)
    out_ref[...] = jnp.zeros_like(out_ref)
    for o in range(span):
        count_ref[o] = 0
    lanes = lax.broadcasted_iota(jnp.int32, (BS, out_ref.shape[1]), 1)
    used = 3 * BS * BS
    spare = jnp.zeros((out_ref.shape[1] - used, count), jnp.bfloat16)

    def one(c):
        wx, wy, wz = hats(pos_ref, c)
        rows = []
        for d in range(3):
            push = force_ref[d, pl.ds(c, 1), :] * stiff_ref[c]
            for x in range(BS):
                rows.append((push * wx[x : x + 1]) * wy)
        high, low = halves(jnp.concatenate(rows, axis=0))
        weights = jnp.concatenate(halves(wz), axis=0)
        first = rows_dot(weights, jnp.concatenate([high, spare], axis=0))
        second = rows_dot(weights, jnp.concatenate([low, spare], axis=0))
        block = first[:BS] + first[BS:] + second[:BS]
        tag = (block_ref[c] + 1).astype(jnp.float32)
        owner = owner_ref[c]
        rank = count_ref[owner]
        count_ref[owner] = rank + 1
        slot = owner * cap + rank
        slot_ref[c] = slot
        out_ref[pl.ds(pl.multiple_of(slot * BS, BS), BS), :] = jnp.where(lanes < used, block, tag)

    grouped(cells, one)


def place_forces(arrived_ref, field_ref, hit_ref):
    _, extent_x, extent_y, extent_z = field_ref.shape
    used = 3 * BS * BS
    slots, width = hit_ref.shape
    tag = arrived_ref[:, used : used + 1]
    row = lax.broadcasted_iota(jnp.int32, (slots, width), 0)
    col = lax.broadcasted_iota(jnp.int32, (slots, width), 1)
    same = (tag - 1.0 == (col // BS).astype(jnp.float32)) & (row % BS == col % BS)
    hit = jnp.where(same, 1.0, 0.0).astype(jnp.bfloat16)
    hit_ref[...] = hit
    high, low = halves(arrived_ref[...].T)
    placed = COUPLING * (plain_dot(high, hit) + plain_dot(low, hit))
    across = extent_y // BS
    for bx in range(extent_x // BS):
        for by in range(across):
            c = bx * across + by
            for d in range(3):
                part = placed[d * BS * BS : (d + 1) * BS * BS, c * extent_z : (c + 1) * extent_z]
                field_ref[d, bx * BS : (bx + 1) * BS, by * BS : (by + 1) * BS, :] = part.reshape(
                    BS, BS, extent_z
                )


def moments(g):
    axis_sum = (g[1] + g[2]) + (g[3] + g[4]) + (g[5] + g[6])
    edge_sum = g[7]
    for q in range(8, Q):
        edge_sum = edge_sum + g[q]
    density = g[0] * (1.0 / 3.0) + axis_sum * (1.0 / 18.0) + edge_sum * (1.0 / 36.0)
    pair = {q: g[q] - g[q + 1] for q in range(1, Q, 2)}
    inverse = 1.0 / density
    velocity = []
    for d in range(3):
        axis, edge = None, None
        for q in range(1, Q, 2):
            sign = LATTICE[q][d]
            if sign == 0:
                continue
            term = pair[q] if sign > 0 else -pair[q]
            if q < 7:
                axis = term
            else:
                edge = term if edge is None else edge + term
        velocity.append((axis * (1.0 / 18.0) + edge * (1.0 / 36.0)) * inverse)
    return density, velocity


def along(c, v):
    total = None
    for d in range(3):
        if c[d] != 0:
            term = v[d] if c[d] > 0 else -v[d]
            total = term if total is None else total + term
    return total


def collide(g, density, velocity, force, omega):
    square = velocity[0] * velocity[0] + velocity[1] * velocity[1] + velocity[2] * velocity[2]
    base = 1.0 - 1.5 * square
    rated = omega * density
    keep = 1.0 - omega
    post = [keep * g[0] + rated * base]
    for q in range(1, Q, 2):
        project = along(LATTICE[q], velocity)
        even = rated * (base + 4.5 * (project * project))
        odd = rated * project
        if force is not None:
            odd = odd + along(LATTICE[q], force)
        odd = 3.0 * odd
        post.append(keep * g[q] + (even + odd))
        post.append(keep * g[q + 1] + (even - odd))
    return post


def flow_kernel(
    span_x, span_y, state_ref, cut_refs, outgoing_ref, up_ref, par_ref, flow_ref, ret_ref,
    load, load_cut, load_sem, arrived, field_ref, hit_ref, p_ref, u_ref, sx, rx, sy, ry, sc, rc, give, take, send_sem, recv_sem, give_sem, take_sem, go_sem, come_sem,
):
    me_x, me_y = lax.axis_index("gx"), lax.axis_index("gy")
    _, extent_x, extent_y, extent_z = state_ref.shape
    halfs = extent_y // BS

    def inside(dx, dy):
        there_x, there_y = me_x + dx, me_y + dy
        return (there_x >= 0) & (there_x < span_x) & (there_y >= 0) & (there_y < span_y)

    def device(dx, dy):
        return (lax.rem(me_x + dx + span_x, span_x), lax.rem(me_y + dy + span_y, span_y))

    barrier = pltpu.get_barrier_semaphore()
    for k in range(1, span_x):
        pl.semaphore_signal(
            barrier, inc=1, device_id=(lax.rem(me_x + k, span_x), me_y), device_id_type=MESH
        )
    for dx, dy in FACES:
        if dy != 0:

            @pl.when(inside(dx, dy))
            def _():
                pl.semaphore_signal(barrier, inc=1, device_id=device(dx, dy), device_id_type=MESH)

    share = give.shape[0] // span_x

    def part(index):
        return pl.ds(pl.multiple_of(index * share, BS), share)

    own = part(me_x)

    def copy_out(src, dst, out_sem, in_sem, k):
        there = lax.rem(me_x + k, span_x)
        return pltpu.make_async_remote_copy(
            src_ref=src.at[part(there)],
            dst_ref=dst.at[own],
            send_sem=out_sem.at[k],
            recv_sem=in_sem.at[k],
            device_id=(there, me_y),
            device_id_type=MESH,
        )

    def copy_in(src, dst, out_sem, in_sem, k):
        there = lax.rem(me_x + span_x - k, span_x)
        return pltpu.make_async_remote_copy(
            src_ref=src.at[part(there)],
            dst_ref=dst.at[part(there)],
            send_sem=out_sem.at[k],
            recv_sem=in_sem.at[k],
            device_id=(there, me_y),
            device_id_type=MESH,
        )

    starts = [0]
    for cut_ref in cut_refs:
        starts.append(starts[-1] + cut_ref.shape[0])
    loads = [pltpu.make_async_copy(state_ref, load, load_sem.at[0])]
    for i, cut_ref in enumerate(cut_refs):
        loads.append(
            pltpu.make_async_copy(
                cut_ref, load_cut.at[starts[i] : starts[i + 1]], load_sem.at[i + 1]
            )
        )
    for copy in loads:
        copy.start()
    u_ref[...] = jnp.zeros_like(u_ref)
    peers = span_x - 1
    for dx, dy in FACES:
        if dy != 0:
            peers = peers + jnp.where(inside(dx, dy), 1, 0)
    pl.semaphore_wait(barrier, peers)
    for k in range(1, span_x):
        copy_out(outgoing_ref, arrived, go_sem, come_sem, k).start()
    arrived[own, :] = outgoing_ref[own, :]

    omega, omega_first, filled = par_ref[0], par_ref[1], par_ref[2]
    inflow = [par_ref[3], par_ref[4], par_ref[5]]
    inflow_square = inflow[0] * inflow[0] + inflow[1] * inflow[1] + inflow[2] * inflow[2]
    ghost = []
    for c in LATTICE:
        project = c[0] * inflow[0] + c[1] * inflow[1] + c[2] * inflow[2]
        ghost.append(1.0 + 3.0 * project + 4.5 * project * project - 1.5 * inflow_square)

    def buffers(turn, face):
        dx, dy = FACES[face]
        if dy == 0:
            return sx.at[turn, face], rx.at[turn, face]
        if dx == 0:
            return sy.at[turn, face - 2], ry.at[turn, face - 2]
        return sc.at[turn, face - 4], rc.at[turn, face - 4]

    def copy_of(turn, face):
        dx, dy = FACES[face]
        src, dst = buffers(turn, face)
        return pltpu.make_async_remote_copy(
            src_ref=src,
            dst_ref=dst,
            send_sem=send_sem.at[turn, face],
            recv_sem=recv_sem.at[turn, face],
            device_id=device(dx, dy),
            device_id_type=MESH,
        )

    def store(turn, x, h, post):
        for q in range(Q):
            p_ref[turn, q, x + 1, PAD + h * BS : PAD + (h + 1) * BS, :] = post[q]
        pack(turn, x, h, post)

    def pack(turn, x, h, post):
        if h == halfs - 1:
            for k, q in enumerate(columns_along(0, 1)):
                sy[turn, 0, k, pl.ds(x, 1), :] = post[q][BS - 1 : BS]
        if h == 0:
            for k, q in enumerate(columns_along(0, -1)):
                sy[turn, 1, k, pl.ds(x, 1), :] = post[q][0:1]

    def send(turn, faces):
        for face in faces:
            dx, dy = FACES[face]
            x = extent_x if dx > 0 else 1
            y = PAD + extent_y - 1 if dy > 0 else PAD
            if dy == 0:
                for k, q in enumerate(columns_along(dx, dy)):
                    sx[turn, face, k] = p_ref[turn, q, x, PAD : PAD + extent_y, :]
            elif dx != 0:
                (q,) = columns_along(dx, dy)
                sc[turn, face - 4] = p_ref[turn, q, x, y : y + 1, :]

            @pl.when(inside(dx, dy))
            def _():
                copy_of(turn, face).start()

    def edges_first(turn, one):
        def outer(i, carry):
            one(i * (extent_x - 1))
            return carry

        def inner(x, carry):
            one(x)
            return carry

        lax.fori_loop(0, 2, outer, 0)
        send(turn, (0, 1, 4, 5, 6, 7))
        lax.fori_loop(1, extent_x - 1, inner, 0)
        send(turn, (2, 3))

    def receive(turn):
        for face, (dx, dy) in enumerate(FACES):
            x = 0 if dx > 0 else extent_x + 1
            y = PAD - 1 if dy > 0 else PAD + extent_y
            columns = columns_along(dx, dy)

            @pl.when(inside(-dx, -dy))
            def _():
                copy_of(turn, face).wait_recv()
                if dy == 0:
                    for k, q in enumerate(columns):
                        p_ref[turn, q, x, PAD : PAD + extent_y, :] = rx[turn, face, k]
                elif dx == 0:
                    for k, q in enumerate(columns):
                        for i in range(extent_x):
                            p_ref[turn, q, i + 1, y : y + 1, :] = ry[turn, face - 2, k, i : i + 1, :]
                else:
                    p_ref[turn, columns[0], x, y : y + 1, :] = rc[turn, face - 4]

            @pl.when(jnp.logical_not(inside(-dx, -dy)))
            def _():
                for q in columns:
                    if dy == 0:
                        p_ref[turn, q, x, PAD : PAD + extent_y, :] = jnp.full(
                            (extent_y, extent_z), ghost[q]
                        )
                    elif dx == 0:
                        for i in range(extent_x):
                            p_ref[turn, q, i + 1, y : y + 1, :] = jnp.full((1, extent_z), ghost[q])
                    else:
                        p_ref[turn, q, x, y : y + 1, :] = jnp.full((1, extent_z), ghost[q])

    def pulled(turn, x, h):
        g = []
        for q, (cx, cy, cz) in enumerate(LATTICE):
            start = PAD + h * BS - cy
            row = p_ref[turn, q, x + 1 - cx, start : start + BS, :]
            if cz != 0:
                row = pltpu.roll(row, cz % extent_z, 1)
            g.append(row)
        return g

    def push_at(x, h):
        return [field_ref[d, x, h * BS : (h + 1) * BS, :] for d in range(3)]

    fresh = jnp.full((BS, extent_z), filled) > 0.5

    for copy in loads:
        copy.wait()

    def first(x, carry):
        for h in range(halfs):
            rows = slice(h * BS, (h + 1) * BS)
            g = [load[q, x, rows, :] + load_cut[q, x, rows, :] for q in range(Q)]
            density, velocity = moments(g)
            coarse = [up_ref[d, x // 2, rows, :] for d in range(4)]
            density = jnp.where(fresh, 1.0 + 0.1 * coarse[0], density)
            velocity = [
                jnp.where(fresh, 0.05 * coarse[d + 1], velocity[d]) for d in range(3)
            ]
            post = collide(g, density, velocity, None, omega_first)
            for q in range(Q):
                p_ref[0, q, x + 1, PAD + h * BS : PAD + (h + 1) * BS, :] = post[q]
        return carry

    lax.fori_loop(0, extent_x, first, 0)
    for k in range(1, span_x):
        copy_in(outgoing_ref, arrived, go_sem, come_sem, k).wait_recv()
    place_forces(arrived, field_ref, hit_ref)

    def pushed(x):
        for h in range(halfs):
            rows = slice(PAD + h * BS, PAD + (h + 1) * BS)
            force = [3.0 * f for f in push_at(x, h)]
            post = [None]
            for q in range(1, Q, 2):
                push = along(LATTICE[q], force)
                post.append(p_ref[0, q, x + 1, rows, :] + push)
                post.append(p_ref[0, q + 1, x + 1, rows, :] - push)
            for q in range(1, Q):
                p_ref[0, q, x + 1, rows, :] = post[q]
            pack(0, x, h, post)

    edges_first(0, pushed)
    receive(0)

    def second(x):
        for h in range(halfs):
            g = pulled(0, x, h)
            density, velocity = moments(g)
            store(1, x, h, collide(g, density, velocity, push_at(x, h), omega))

    edges_first(1, second)
    receive(1)

    for bx in range(extent_x // BS):

        def third(i, carry):
            x = bx * BS + i
            for h in range(halfs):
                g = pulled(1, x, h)
                for q in range(Q):
                    flow_ref[q, x, h * BS : (h + 1) * BS, :] = g[q]
                _, velocity = moments(g)
                c = bx * halfs + h
                for d in range(3):
                    u_ref[
                        pl.ds(pl.multiple_of(d * BS * BS + i * BS, BS), BS),
                        c * extent_z : (c + 1) * extent_z,
                    ] = velocity[d]
            return carry

        lax.fori_loop(0, BS, third, 0)

    high, low = halves(u_ref[...])
    hit = hit_ref[...]
    give[...] = rows_dot(hit, high) + rows_dot(hit, low)

    for k in range(1, span_x):
        copy_out(give, take, give_sem, take_sem, k).start()
    take[own, :] = give[own, :]
    for turn in range(2):
        for face, (dx, dy) in enumerate(FACES):

            @pl.when(inside(dx, dy))
            def _():
                copy_of(turn, face).wait_send()

    for k in range(1, span_x):
        copy_out(give, take, give_sem, take_sem, k).wait_send()
        copy_in(give, take, give_sem, take_sem, k).wait_recv()
        copy_out(outgoing_ref, arrived, go_sem, come_sem, k).wait_send()
    ret_ref[...] = take[...]


def sample_kernel(ret_ref, slot_ref, pos_ref, flow_ref, out_ref, flow_out_ref, sem):
    copy = pltpu.make_async_copy(flow_ref, flow_out_ref, sem)
    copy.start()

    def one(c):
        wx, wy, wz = hats(pos_ref, c)
        slot = slot_ref[c]
        block = ret_ref[pl.ds(pl.multiple_of(slot * BS, BS), BS), :]
        high = block.astype(jnp.bfloat16).astype(jnp.float32)
        left = jnp.concatenate([high, high, block - high], axis=0).T.astype(jnp.bfloat16)
        near = wz.astype(jnp.bfloat16).astype(jnp.float32)
        right = jnp.concatenate([near, wz - near, near], axis=0).astype(jnp.bfloat16)
        lines = plain_dot(left[: 3 * BS * BS], right)
        for d in range(3):
            total = None
            for x in range(BS):
                start = (d * BS + x) * BS
                term = wx[x : x + 1] * lines[start : start + BS]
                total = term if total is None else total + term
            out_ref[d, pl.ds(c, 1), :] = VELOCITY_UNIT * jnp.sum(total * wy, axis=0, keepdims=True)

    grouped(pos_ref.shape[1], one)
    copy.wait()


VMEM = pl.BlockSpec(memory_space=pltpu.VMEM)
ANY = pl.BlockSpec(memory_space=pl.ANY)
SMEM = pl.BlockSpec(memory_space=pltpu.SMEM)


CUTS = (0, 10, 13, 19)


def routes_of(mesh):
    line = list(mesh.devices[:, 0])
    span = len(line)
    places = []
    for device in line:
        coords = getattr(device, "coords", None)
        if coords is None:
            return {s: ([(i, i - s) for i in range(s, span)], [], [], [], (0, 0, 0)) for s in range(1, span)}
        places.append((coords[0], coords[1], getattr(device, "core_on_chip", 0)))
    routes = {}
    for s in range(1, span):
        pairs = [(i, i - s) for i in range(s, span)]
        turning, hop, onward = [], [], []
        for i, j in pairs:
            corner = (places[j][0], places[i][1], places[j][2])
            if places[i][0] != places[j][0] and places[i][1] != places[j][1] and corner in places:
                relay = places.index(corner)
                turning.append((i, j))
                hop.append((i, relay))
                onward.append((relay, j))
        plain = [pair for pair in pairs if pair not in turning]
        load = {}
        for i, j in plain:
            leg = places[i][:2] + places[j][:2]
            load[leg] = load.get(leg, 0) + 1
        crowded = any(places[i][:2] + places[j][:2] in load for i, j in hop)
        relays = [j for _, j in hop]
        idle = not turning or (plain and not crowded)
        if len(set(relays)) < len(relays) or max(load.values(), default=0) > 1 or idle:
            routes[s] = (pairs, [], [], [], (0, 0, 0))
        elif crowded:
            routes[s] = (plain, turning, hop, onward, (0, 1, 1))
        else:
            routes[s] = (plain, turning, hop, onward, (0, 0, 1))
    return routes


def body(
    routes,
    populations,
    coarse_state,
    window_shift,
    inflow,
    relaxation,
    positions,
    rest_shape,
    stiffness,
    cell_owner,
    cell_block,
    triangles,
):
    span_x = lax.axis_size("gx")
    span_y = lax.axis_size("gy")
    here_x = lax.axis_index("gx")
    _, extent_x, extent_y, extent_z = populations.shape
    cells, _, count = positions.shape
    positions = positions.transpose(1, 0, 2)
    cap = 2 * cells // span_x
    slots = span_x * cap
    width = 256
    blocks = extent_x // BS * (extent_y // BS) * (extent_z // BS)
    f32 = jnp.float32
    shift = window_shift[0]

    def cell_part(positions, rest_shape, stiffness, owner, block, triangles, coarse):
        return pl.pallas_call(
            functools.partial(spread_kernel, span_x, cap),
            out_shape=(
                jax.ShapeDtypeStruct((slots * BS, width), f32),
                jax.ShapeDtypeStruct((cells,), jnp.int32),
                jax.ShapeDtypeStruct((4, extent_x // 2, extent_y, extent_z), f32),
            ),
            in_specs=[VMEM, VMEM, SMEM, SMEM, SMEM, VMEM, VMEM],
            out_specs=(VMEM, SMEM, VMEM),
            scratch_shapes=[
                pltpu.VMEM((3, cells, count), f32),
                pltpu.SMEM((span_x,), jnp.int32),
            ],
            compiler_params=pltpu.CompilerParams(vmem_limit_bytes=48 << 20),
            cost_estimate=pl.CostEstimate(
                flops=2_000_000_000, bytes_accessed=4_000_000, transcendentals=0
            ),
            name="spread",
        )(positions, rest_shape, stiffness, owner, block, triangles, coarse)

    def moved_by(distance, populations, *rest):
        plain, turning, hop, onward, ways = routes[distance]
        lengths = [end - begin for begin, end in zip(CUTS, CUTS[1:])]
        whole = cuts = None
        if plain:
            whole = lax.ppermute(populations, "gx", plain)
        else:
            whole = jnp.zeros_like(populations)
            whole, rest = lax.optimization_barrier((whole, rest))
        if not turning:
            cuts = tuple(jnp.zeros((length,) + populations.shape[1:], f32) for length in lengths)
            cuts, rest = lax.optimization_barrier((cuts, rest))
        outgoing, slot, up = cell_part(*rest)
        if not turning:
            return whole, cuts, outgoing, slot, up
        cuts = []
        for begin, end, way in zip(CUTS, CUTS[1:], ways):
            cut = populations[begin:end]
            if way:
                cut, outgoing = lax.optimization_barrier((lax.ppermute(cut, "gx", hop), outgoing))
                cut = lax.ppermute(cut, "gx", onward)
            else:
                cut = lax.ppermute(cut, "gx", turning)
            cuts.append(cut)
        return whole, tuple(cuts), outgoing, slot, up

    coarse = coarse_state.reshape(-1, coarse_state.shape[3])
    whole, cuts, outgoing, slot, up = lax.switch(
        shift - 1,
        [functools.partial(moved_by, distance) for distance in range(1, span_x)],
        populations,
        positions,
        rest_shape,
        stiffness,
        cell_owner[:, 0],
        cell_block,
        triangles,
        coarse,
    )
    entering = here_x + shift >= span_x
    omega = relaxation[0]
    par = jnp.concatenate(
        [
            jnp.stack([omega, jnp.where(entering, 1.0, omega), jnp.where(entering, 1.0, 0.0)]),
            inflow,
        ]
    )
    faces = len(FACES)
    flow, ret = pl.pallas_call(
        functools.partial(flow_kernel, span_x, span_y),
        out_shape=(
            jax.ShapeDtypeStruct(populations.shape, f32),
            jax.ShapeDtypeStruct((slots * BS, width), f32),
        ),
        in_specs=[ANY, [ANY] * len(cuts), VMEM, VMEM, SMEM],
        out_specs=(VMEM, VMEM),
        scratch_shapes=[
            pltpu.VMEM(populations.shape, f32),
            pltpu.VMEM(populations.shape, f32),
            pltpu.SemaphoreType.DMA((1 + len(cuts),)),
            pltpu.VMEM((slots * BS, width), f32),
            pltpu.VMEM((3, extent_x, extent_y, extent_z), f32),
            pltpu.VMEM((slots * BS, blocks * BS), jnp.bfloat16),
            pltpu.VMEM((2, Q, extent_x + 2, extent_y + 2 * PAD, extent_z), f32),
            pltpu.VMEM((width, blocks * BS), f32),
            pltpu.VMEM((2, 2, 5, extent_y, extent_z), f32),
            pltpu.VMEM((2, 2, 5, extent_y, extent_z), f32),
            pltpu.VMEM((2, 2, 5, extent_x, extent_z), f32),
            pltpu.VMEM((2, 2, 5, extent_x, extent_z), f32),
            pltpu.VMEM((2, 4, 1, extent_z), f32),
            pltpu.VMEM((2, 4, 1, extent_z), f32),
            pltpu.VMEM((slots * BS, width), f32),
            pltpu.VMEM((slots * BS, width), f32),
            pltpu.SemaphoreType.DMA((2, faces)),
            pltpu.SemaphoreType.DMA((2, faces)),
            pltpu.SemaphoreType.DMA((span_x,)),
            pltpu.SemaphoreType.DMA((span_x,)),
            pltpu.SemaphoreType.DMA((span_x,)),
            pltpu.SemaphoreType.DMA((span_x,)),
        ],
        compiler_params=pltpu.CompilerParams(
            collective_id=0, has_side_effects=True, vmem_limit_bytes=48 << 20
        ),
        cost_estimate=pl.CostEstimate(
            flops=100_000_000, bytes_accessed=8_000_000, transcendentals=0
        ),
        name="flow",
    )(whole, list(cuts), outgoing, up, par)
    cell_velocity, flow = pl.pallas_call(
        sample_kernel,
        out_shape=(
            jax.ShapeDtypeStruct(positions.shape, f32),
            jax.ShapeDtypeStruct(populations.shape, f32),
        ),
        in_specs=[VMEM, SMEM, VMEM, ANY],
        out_specs=(VMEM, ANY),
        scratch_shapes=[pltpu.SemaphoreType.DMA],
        compiler_params=pltpu.CompilerParams(vmem_limit_bytes=48 << 20),
        cost_estimate=pl.CostEstimate(
            flops=200_000_000, bytes_accessed=1_000_000, transcendentals=0
        ),
        name="sample",
    )(ret, slot, positions, flow)
    return (flow, cell_velocity.transpose(1, 0, 2))


def solution(mesh):
    placed = (
        P(None, "gx", "gy", None),
        P(None, "gx", "gy", None),
        P(),
        P(),
        P(),
        P(("gx", "gy"), None, None),
        P(),
        P(("gx", "gy")),
        P(("gx", "gy"), None),
        P(("gx", "gy")),
        P(),
    )
    return jax.shard_map(
        functools.partial(body, routes_of(mesh)),
        mesh=mesh,
        in_specs=placed,
        out_specs=(P(None, "gx", "gy", None), P(("gx", "gy"), None, None)),
        check_vma=False,
    )
```

```python
import functools
import jax
import jax.numpy as jnp
from jax import lax
from jax.experimental import pallas as pl
from jax.experimental.pallas import tpu as pltpu
from jax.sharding import PartitionSpec as P

BS = 8
LATTICE = (
    (0, 0, 0),
    (1, 0, 0),
    (-1, 0, 0),
    (0, 1, 0),
    (0, -1, 0),
    (0, 0, 1),
    (0, 0, -1),
    (1, 1, 0),
    (-1, -1, 0),
    (1, -1, 0),
    (-1, 1, 0),
    (1, 0, 1),
    (-1, 0, -1),
    (1, 0, -1),
    (-1, 0, 1),
    (0, 1, 1),
    (0, -1, -1),
    (0, 1, -1),
    (0, -1, 1),
)
Q = len(LATTICE)
COUPLING = 0.001
VELOCITY_UNIT = 20.0
HIGHEST = lax.Precision.HIGHEST
MESH = pl.DeviceIdType.MESH
PAD = 8
FACES = ((1, 0), (-1, 0), (0, 1), (0, -1), (1, 1), (-1, -1), (1, -1), (-1, 1))


def columns_along(dx, dy):
    return [
        q
        for q, (cx, cy, _) in enumerate(LATTICE)
        if (dx == 0 or cx == dx) and (dy == 0 or cy == dy)
    ]


def halves(x):
    high = x.astype(jnp.bfloat16)
    low = (x - high.astype(jnp.float32)).astype(jnp.bfloat16)
    return high, low


def rows_dot(a, b):
    return lax.dot_general(a, b, (((1,), (1,)), ((), ())), preferred_element_type=jnp.float32)


def plain_dot(a, b):
    return lax.dot_general(a, b, (((1,), (0,)), ((), ())), preferred_element_type=jnp.float32)


def grouped(number, one):
    size = 4 if number % 4 == 0 else 1

    def group(i, carry):
        for j in range(size):
            one(i * size + j)
        return carry

    lax.fori_loop(0, number // size, group, 0)


def hats(pos_ref, c):
    nodes = lax.broadcasted_iota(jnp.int32, (BS, pos_ref.shape[2]), 0).astype(jnp.float32)
    return [
        jnp.maximum(0.0, 1.0 - jnp.abs(pos_ref[d, pl.ds(c, 1), :] - nodes)) for d in range(3)
    ]


def spread_kernel(
    span, cap, early_refs, pos_ref, rest_ref, stiff_ref, owner_ref, block_ref, tri_ref, coarse_ref,
    out_ref, slot_ref, up_ref, force_ref, count_ref,
):
    _, cells, count = pos_ref.shape
    tri = tri_ref[...]
    vertices = lax.broadcasted_iota(jnp.int32, (tri.shape[0], count), 1)
    hit = (tri[:, 0:1] == vertices) | (tri[:, 1:2] == vertices) | (tri[:, 2:3] == vertices)
    member = jnp.where(hit, 1.0, 0.0)
    degree = jnp.sum(member, axis=0, keepdims=True)
    member = member.astype(jnp.bfloat16)
    gap = jnp.concatenate([pos_ref[d] - rest_ref[d : d + 1, :] for d in range(3)], axis=0)
    high, low = halves(gap)
    each = rows_dot(high, member) + rows_dot(low, member)
    high, low = halves(each)
    back = plain_dot(high, member) + plain_dot(low, member)
    force_ref[...] = (back - 3.0 * degree * gap).reshape(3, cells, count)
    coarse = coarse_ref[...]
    rows, depth = coarse.shape
    extent_z = up_ref.shape[3]
    pick_z = jnp.where(
        lax.broadcasted_iota(jnp.int32, (depth, extent_z), 1) // 2
        == lax.broadcasted_iota(jnp.int32, (depth, extent_z), 0),
        1.0,
        0.0,
    )
    pick_y = jnp.where(
        lax.broadcasted_iota(jnp.int32, (2 * rows, rows), 0) // 2
        == lax.broadcasted_iota(jnp.int32, (2 * rows, rows), 1),
        1.0,
        0.0,
    )
    along = jnp.dot(coarse, pick_z, precision=HIGHEST, preferred_element_type=jnp.float32)
    wide = jnp.dot(pick_y, along, precision=HIGHEST, preferred_element_type=jnp.float32)
    up_ref[...] = wide.reshape(up_ref.shape)
    out_ref[...] = jnp.zeros_like(out_ref)
    for o in range(span):
        count_ref[o] = 0
    lanes = lax.broadcasted_iota(jnp.int32, (BS, out_ref.shape[1]), 1)
    used = 3 * BS * BS
    spare = jnp.zeros((out_ref.shape[1] - used, count), jnp.bfloat16)

    def one(c):
        wx, wy, wz = hats(pos_ref, c)
        rows = []
        for d in range(3):
            push = force_ref[d, pl.ds(c, 1), :] * stiff_ref[c]
            for x in range(BS):
                rows.append((push * wx[x : x + 1]) * wy)
        high, low = halves(jnp.concatenate(rows, axis=0))
        weights = jnp.concatenate(halves(wz), axis=0)
        first = rows_dot(weights, jnp.concatenate([high, spare], axis=0))
        second = rows_dot(weights, jnp.concatenate([low, spare], axis=0))
        block = first[:BS] + first[BS:] + second[:BS]
        tag = (block_ref[c] + 1).astype(jnp.float32)
        owner = owner_ref[c]
        rank = count_ref[owner]
        count_ref[owner] = rank + 1
        slot = owner * cap + rank
        slot_ref[c] = slot
        out_ref[pl.ds(pl.multiple_of(slot * BS, BS), BS), :] = jnp.where(lanes < used, block, tag)

    grouped(cells, one)


def place_forces(arrived_ref, field_ref, hit_ref):
    _, extent_x, extent_y, extent_z = field_ref.shape
    used = 3 * BS * BS
    slots, width = hit_ref.shape
    tag = arrived_ref[:, used : used + 1]
    row = lax.broadcasted_iota(jnp.int32, (slots, width), 0)
    col = lax.broadcasted_iota(jnp.int32, (slots, width), 1)
    same = (tag - 1.0 == (col // BS).astype(jnp.float32)) & (row % BS == col % BS)
    hit = jnp.where(same, 1.0, 0.0).astype(jnp.bfloat16)
    hit_ref[...] = hit
    high, low = halves(arrived_ref[...].T)
    placed = COUPLING * (plain_dot(high, hit) + plain_dot(low, hit))
    across = extent_y // BS
    for bx in range(extent_x // BS):
        for by in range(across):
            c = bx * across + by
            for d in range(3):
                part = placed[d * BS * BS : (d + 1) * BS * BS, c * extent_z : (c + 1) * extent_z]
                field_ref[d, bx * BS : (bx + 1) * BS, by * BS : (by + 1) * BS, :] = part.reshape(
                    BS, BS, extent_z
                )


def moments(g):
    axis_sum = (g[1] + g[2]) + (g[3] + g[4]) + (g[5] + g[6])
    edge_sum = g[7]
    for q in range(8, Q):
        edge_sum = edge_sum + g[q]
    density = g[0] * (1.0 / 3.0) + axis_sum * (1.0 / 18.0) + edge_sum * (1.0 / 36.0)
    pair = {q: g[q] - g[q + 1] for q in range(1, Q, 2)}
    inverse = 1.0 / density
    velocity = []
    for d in range(3):
        axis, edge = None, None
        for q in range(1, Q, 2):
            sign = LATTICE[q][d]
            if sign == 0:
                continue
            term = pair[q] if sign > 0 else -pair[q]
            if q < 7:
                axis = term
            else:
                edge = term if edge is None else edge + term
        velocity.append((axis * (1.0 / 18.0) + edge * (1.0 / 36.0)) * inverse)
    return density, velocity


def along(c, v):
    total = None
    for d in range(3):
        if c[d] != 0:
            term = v[d] if c[d] > 0 else -v[d]
            total = term if total is None else total + term
    return total


def collide(g, density, velocity, force, omega):
    square = velocity[0] * velocity[0] + velocity[1] * velocity[1] + velocity[2] * velocity[2]
    base = 1.0 - 1.5 * square
    rated = omega * density
    keep = 1.0 - omega
    post = [keep * g[0] + rated * base]
    for q in range(1, Q, 2):
        project = along(LATTICE[q], velocity)
        even = rated * (base + 4.5 * (project * project))
        odd = rated * project
        if force is not None:
            odd = odd + along(LATTICE[q], force)
        odd = 3.0 * odd
        post.append(keep * g[q] + (even + odd))
        post.append(keep * g[q + 1] + (even - odd))
    return post


def flow_kernel(
    span_x, span_y, state_ref, cut_refs, outgoing_ref, up_ref, par_ref, flow_ref, ret_ref,
    load, load_cut, load_sem, arrived, field_ref, hit_ref, p_ref, u_ref, sx, rx, sy, ry, sc, rc, give, take, send_sem, recv_sem, give_sem, take_sem, go_sem, come_sem,
):
    me_x, me_y = lax.axis_index("gx"), lax.axis_index("gy")
    _, extent_x, extent_y, extent_z = state_ref.shape
    halfs = extent_y // BS

    def inside(dx, dy):
        there_x, there_y = me_x + dx, me_y + dy
        return (there_x >= 0) & (there_x < span_x) & (there_y >= 0) & (there_y < span_y)

    def device(dx, dy):
        return (lax.rem(me_x + dx + span_x, span_x), lax.rem(me_y + dy + span_y, span_y))

    barrier = pltpu.get_barrier_semaphore()
    for k in range(1, span_x):
        pl.semaphore_signal(
            barrier, inc=1, device_id=(lax.rem(me_x + k, span_x), me_y), device_id_type=MESH
        )
    for dx, dy in FACES:
        if dy != 0:

            @pl.when(inside(dx, dy))
            def _():
                pl.semaphore_signal(barrier, inc=1, device_id=device(dx, dy), device_id_type=MESH)

    share = give.shape[0] // span_x

    def part(index):
        return pl.ds(pl.multiple_of(index * share, BS), share)

    own = part(me_x)

    def copy_out(src, dst, out_sem, in_sem, k):
        there = lax.rem(me_x + k, span_x)
        return pltpu.make_async_remote_copy(
            src_ref=src.at[part(there)],
            dst_ref=dst.at[own],
            send_sem=out_sem.at[k],
            recv_sem=in_sem.at[k],
            device_id=(there, me_y),
            device_id_type=MESH,
        )

    def copy_in(src, dst, out_sem, in_sem, k):
        there = lax.rem(me_x + span_x - k, span_x)
        return pltpu.make_async_remote_copy(
            src_ref=src.at[part(there)],
            dst_ref=dst.at[part(there)],
            send_sem=out_sem.at[k],
            recv_sem=in_sem.at[k],
            device_id=(there, me_y),
            device_id_type=MESH,
        )

    starts = [0]
    for cut_ref in cut_refs:
        starts.append(starts[-1] + cut_ref.shape[0])
    loads = [pltpu.make_async_copy(state_ref, load, load_sem.at[0])]
    for i, cut_ref in enumerate(cut_refs):
        loads.append(
            pltpu.make_async_copy(
                cut_ref, load_cut.at[starts[i] : starts[i + 1]], load_sem.at[i + 1]
            )
        )
    for copy in loads:
        copy.start()
    u_ref[...] = jnp.zeros_like(u_ref)
    peers = span_x - 1
    for dx, dy in FACES:
        if dy != 0:
            peers = peers + jnp.where(inside(dx, dy), 1, 0)
    pl.semaphore_wait(barrier, peers)
    for k in range(1, span_x):
        copy_out(outgoing_ref, arrived, go_sem, come_sem, k).start()
    arrived[own, :] = outgoing_ref[own, :]

    omega, omega_first, filled = par_ref[0], par_ref[1], par_ref[2]
    inflow = [par_ref[3], par_ref[4], par_ref[5]]
    inflow_square = inflow[0] * inflow[0] + inflow[1] * inflow[1] + inflow[2] * inflow[2]
    ghost = []
    for c in LATTICE:
        project = c[0] * inflow[0] + c[1] * inflow[1] + c[2] * inflow[2]
        ghost.append(1.0 + 3.0 * project + 4.5 * project * project - 1.5 * inflow_square)

    def buffers(turn, face):
        dx, dy = FACES[face]
        if dy == 0:
            return sx.at[turn, face], rx.at[turn, face]
        if dx == 0:
            return sy.at[turn, face - 2], ry.at[turn, face - 2]
        return sc.at[turn, face - 4], rc.at[turn, face - 4]

    def copy_of(turn, face):
        dx, dy = FACES[face]
        src, dst = buffers(turn, face)
        return pltpu.make_async_remote_copy(
            src_ref=src,
            dst_ref=dst,
            send_sem=send_sem.at[turn, face],
            recv_sem=recv_sem.at[turn, face],
            device_id=device(dx, dy),
            device_id_type=MESH,
        )

    def store(turn, x, h, post):
        for q in range(Q):
            p_ref[turn, q, x + 1, PAD + h * BS : PAD + (h + 1) * BS, :] = post[q]
        pack(turn, x, h, post)

    def pack(turn, x, h, post):
        if h == halfs - 1:
            for k, q in enumerate(columns_along(0, 1)):
                sy[turn, 0, k, pl.ds(x, 1), :] = post[q][BS - 1 : BS]
        if h == 0:
            for k, q in enumerate(columns_along(0, -1)):
                sy[turn, 1, k, pl.ds(x, 1), :] = post[q][0:1]

    def send(turn, faces):
        for face in faces:
            dx, dy = FACES[face]
            x = extent_x if dx > 0 else 1
            y = PAD + extent_y - 1 if dy > 0 else PAD
            if dy == 0:
                for k, q in enumerate(columns_along(dx, dy)):
                    sx[turn, face, k] = p_ref[turn, q, x, PAD : PAD + extent_y, :]
            elif dx != 0:
                (q,) = columns_along(dx, dy)
                sc[turn, face - 4] = p_ref[turn, q, x, y : y + 1, :]

            @pl.when(inside(dx, dy))
            def _():
                copy_of(turn, face).start()

    def edges_first(turn, one):
        def outer(i, carry):
            one(i * (extent_x - 1))
            return carry

        def inner(x, carry):
            one(x)
            return carry

        lax.fori_loop(0, 2, outer, 0)
        send(turn, (0, 1, 4, 5, 6, 7))
        lax.fori_loop(1, extent_x - 1, inner, 0)
        send(turn, (2, 3))

    def receive(turn):
        for face, (dx, dy) in enumerate(FACES):
            x = 0 if dx > 0 else extent_x + 1
            y = PAD - 1 if dy > 0 else PAD + extent_y
            columns = columns_along(dx, dy)

            @pl.when(inside(-dx, -dy))
            def _():
                copy_of(turn, face).wait_recv()
                if dy == 0:
                    for k, q in enumerate(columns):
                        p_ref[turn, q, x, PAD : PAD + extent_y, :] = rx[turn, face, k]
                elif dx == 0:
                    for k, q in enumerate(columns):
                        for i in range(extent_x):
                            p_ref[turn, q, i + 1, y : y + 1, :] = ry[turn, face - 2, k, i : i + 1, :]
                else:
                    p_ref[turn, columns[0], x, y : y + 1, :] = rc[turn, face - 4]

            @pl.when(jnp.logical_not(inside(-dx, -dy)))
            def _():
                for q in columns:
                    if dy == 0:
                        p_ref[turn, q, x, PAD : PAD + extent_y, :] = jnp.full(
                            (extent_y, extent_z), ghost[q]
                        )
                    elif dx == 0:
                        for i in range(extent_x):
                            p_ref[turn, q, i + 1, y : y + 1, :] = jnp.full((1, extent_z), ghost[q])
                    else:
                        p_ref[turn, q, x, y : y + 1, :] = jnp.full((1, extent_z), ghost[q])

    def pulled(turn, x, h):
        g = []
        for q, (cx, cy, cz) in enumerate(LATTICE):
            start = PAD + h * BS - cy
            row = p_ref[turn, q, x + 1 - cx, start : start + BS, :]
            if cz != 0:
                row = pltpu.roll(row, cz % extent_z, 1)
            g.append(row)
        return g

    def push_at(x, h):
        return [field_ref[d, x, h * BS : (h + 1) * BS, :] for d in range(3)]

    fresh = jnp.full((BS, extent_z), filled) > 0.5

    for copy in loads:
        copy.wait()

    def first(x, carry):
        for h in range(halfs):
            rows = slice(h * BS, (h + 1) * BS)
            g = [load[q, x, rows, :] + load_cut[q, x, rows, :] for q in range(Q)]
            density, velocity = moments(g)
            coarse = [up_ref[d, x // 2, rows, :] for d in range(4)]
            density = jnp.where(fresh, 1.0 + 0.1 * coarse[0], density)
            velocity = [
                jnp.where(fresh, 0.05 * coarse[d + 1], velocity[d]) for d in range(3)
            ]
            post = collide(g, density, velocity, None, omega_first)
            for q in range(Q):
                p_ref[0, q, x + 1, PAD + h * BS : PAD + (h + 1) * BS, :] = post[q]
        return carry

    lax.fori_loop(0, extent_x, first, 0)
    for k in range(1, span_x):
        copy_in(outgoing_ref, arrived, go_sem, come_sem, k).wait_recv()
    place_forces(arrived, field_ref, hit_ref)

    def pushed(x):
        for h in range(halfs):
            rows = slice(PAD + h * BS, PAD + (h + 1) * BS)
            force = [3.0 * f for f in push_at(x, h)]
            post = [None]
            for q in range(1, Q, 2):
                push = along(LATTICE[q], force)
                post.append(p_ref[0, q, x + 1, rows, :] + push)
                post.append(p_ref[0, q + 1, x + 1, rows, :] - push)
            for q in range(1, Q):
                p_ref[0, q, x + 1, rows, :] = post[q]
            pack(0, x, h, post)

    edges_first(0, pushed)
    receive(0)

    def second(x):
        for h in range(halfs):
            g = pulled(0, x, h)
            density, velocity = moments(g)
            store(1, x, h, collide(g, density, velocity, push_at(x, h), omega))

    edges_first(1, second)
    receive(1)

    for bx in range(extent_x // BS):

        def third(i, carry):
            x = bx * BS + i
            for h in range(halfs):
                g = pulled(1, x, h)
                for q in range(Q):
                    flow_ref[q, x, h * BS : (h + 1) * BS, :] = g[q]
                _, velocity = moments(g)
                c = bx * halfs + h
                for d in range(3):
                    u_ref[
                        pl.ds(pl.multiple_of(d * BS * BS + i * BS, BS), BS),
                        c * extent_z : (c + 1) * extent_z,
                    ] = velocity[d]
            return carry

        lax.fori_loop(0, BS, third, 0)

    high, low = halves(u_ref[...])
    hit = hit_ref[...]
    give[...] = rows_dot(hit, high) + rows_dot(hit, low)

    for k in range(1, span_x):
        copy_out(give, take, give_sem, take_sem, k).start()
    take[own, :] = give[own, :]
    for turn in range(2):
        for face, (dx, dy) in enumerate(FACES):

            @pl.when(inside(dx, dy))
            def _():
                copy_of(turn, face).wait_send()

    for k in range(1, span_x):
        copy_out(give, take, give_sem, take_sem, k).wait_send()
        copy_in(give, take, give_sem, take_sem, k).wait_recv()
        copy_out(outgoing_ref, arrived, go_sem, come_sem, k).wait_send()
    ret_ref[...] = take[...]


def sample_kernel(ret_ref, slot_ref, pos_ref, flow_ref, out_ref, flow_out_ref, sem):
    copy = pltpu.make_async_copy(flow_ref, flow_out_ref, sem)
    copy.start()

    def one(c):
        wx, wy, wz = hats(pos_ref, c)
        slot = slot_ref[c]
        block = ret_ref[pl.ds(pl.multiple_of(slot * BS, BS), BS), :]
        high = block.astype(jnp.bfloat16).astype(jnp.float32)
        left = jnp.concatenate([high, high, block - high], axis=0).T.astype(jnp.bfloat16)
        near = wz.astype(jnp.bfloat16).astype(jnp.float32)
        right = jnp.concatenate([near, wz - near, near], axis=0).astype(jnp.bfloat16)
        lines = plain_dot(left[: 3 * BS * BS], right)
        for d in range(3):
            total = None
            for x in range(BS):
                start = (d * BS + x) * BS
                term = wx[x : x + 1] * lines[start : start + BS]
                total = term if total is None else total + term
            out_ref[d, pl.ds(c, 1), :] = VELOCITY_UNIT * jnp.sum(total * wy, axis=0, keepdims=True)

    grouped(pos_ref.shape[1], one)
    copy.wait()


VMEM = pl.BlockSpec(memory_space=pltpu.VMEM)
ANY = pl.BlockSpec(memory_space=pl.ANY)
SMEM = pl.BlockSpec(memory_space=pltpu.SMEM)


CUTS = (0, 10, 13, 19)


def routes_of(mesh):
    line = list(mesh.devices[:, 0])
    span = len(line)
    places = []
    for device in line:
        coords = getattr(device, "coords", None)
        if coords is None:
            return {s: ([(i, i - s) for i in range(s, span)], [], [], [], (0, 0, 0)) for s in range(1, span)}
        places.append((coords[0], coords[1], getattr(device, "core_on_chip", 0)))
    routes = {}
    for s in range(1, span):
        pairs = [(i, i - s) for i in range(s, span)]
        turning, hop, onward = [], [], []
        for i, j in pairs:
            corner = (places[i][0], places[j][1], places[j][2])
            if places[i][0] != places[j][0] and places[i][1] != places[j][1] and corner in places:
                relay = places.index(corner)
                turning.append((i, j))
                hop.append((i, relay))
                onward.append((relay, j))
        plain = [pair for pair in pairs if pair not in turning]
        load = {}
        for i, j in plain:
            leg = places[i][:2] + places[j][:2]
            load[leg] = load.get(leg, 0) + 1
        crowded = any(places[i][:2] + places[j][:2] in load for i, j in hop)
        relays = [j for _, j in hop]
        idle = not turning or (plain and not crowded)
        if len(set(relays)) < len(relays) or max(load.values(), default=0) > 1 or idle:
            routes[s] = (pairs, [], [], [], (0, 0, 0))
        elif crowded:
            routes[s] = (plain, turning, hop, onward, (0, 1, 1))
        else:
            routes[s] = (plain, turning, hop, onward, (0, 0, 1))
    return routes


def body(
    routes,
    populations,
    coarse_state,
    window_shift,
    inflow,
    relaxation,
    positions,
    rest_shape,
    stiffness,
    cell_owner,
    cell_block,
    triangles,
):
    span_x = lax.axis_size("gx")
    span_y = lax.axis_size("gy")
    here_x = lax.axis_index("gx")
    _, extent_x, extent_y, extent_z = populations.shape
    cells, _, count = positions.shape
    positions = positions.transpose(1, 0, 2)
    cap = 2 * cells // span_x
    slots = span_x * cap
    width = 256
    blocks = extent_x // BS * (extent_y // BS) * (extent_z // BS)
    f32 = jnp.float32
    shift = window_shift[0]

    def cell_part(early, positions, rest_shape, stiffness, owner, block, triangles, coarse):
        return pl.pallas_call(
            functools.partial(spread_kernel, span_x, cap),
            out_shape=(
                jax.ShapeDtypeStruct((slots * BS, width), f32),
                jax.ShapeDtypeStruct((cells,), jnp.int32),
                jax.ShapeDtypeStruct((4, extent_x // 2, extent_y, extent_z), f32),
            ),
            in_specs=[[ANY] * len(early), VMEM, VMEM, SMEM, SMEM, SMEM, VMEM, VMEM],
            out_specs=(VMEM, SMEM, VMEM),
            scratch_shapes=[
                pltpu.VMEM((3, cells, count), f32),
                pltpu.SMEM((span_x,), jnp.int32),
            ],
            compiler_params=pltpu.CompilerParams(vmem_limit_bytes=48 << 20),
            cost_estimate=pl.CostEstimate(
                flops=2_000_000_000, bytes_accessed=4_000_000, transcendentals=0
            ),
            name="spread",
        )(early, positions, rest_shape, stiffness, owner, block, triangles, coarse)

    def moved_by(distance, populations, *rest):
        plain, turning, hop, onward, ways = routes[distance]
        lengths = [end - begin for begin, end in zip(CUTS, CUTS[1:])]
        early = []
        if plain:
            whole = lax.ppermute(populations, "gx", plain)
        else:
            whole = jnp.zeros_like(populations)
            early.append(whole)
        if not turning:
            cuts = tuple(jnp.zeros((length,) + populations.shape[1:], f32) for length in lengths)
            early.extend(cuts)
        outgoing, slot, up = cell_part(early, *rest)
        if not turning:
            return whole, cuts, outgoing, slot, up
        cuts = []
        for begin, end, way in zip(CUTS, CUTS[1:], ways):
            cut = populations[begin:end]
            if way:
                cut, outgoing = lax.optimization_barrier((lax.ppermute(cut, "gx", hop), outgoing))
                cut = lax.ppermute(cut, "gx", onward)
            else:
                cut = lax.ppermute(cut, "gx", turning)
            cuts.append(cut)
        return whole, tuple(cuts), outgoing, slot, up

    coarse = coarse_state.reshape(-1, coarse_state.shape[3])
    whole, cuts, outgoing, slot, up = lax.switch(
        shift - 1,
        [functools.partial(moved_by, distance) for distance in range(1, span_x)],
        populations,
        positions,
        rest_shape,
        stiffness,
        cell_owner[:, 0],
        cell_block,
        triangles,
        coarse,
    )
    entering = here_x + shift >= span_x
    omega = relaxation[0]
    par = jnp.concatenate(
        [
            jnp.stack([omega, jnp.where(entering, 1.0, omega), jnp.where(entering, 1.0, 0.0)]),
            inflow,
        ]
    )
    faces = len(FACES)
    flow, ret = pl.pallas_call(
        functools.partial(flow_kernel, span_x, span_y),
        out_shape=(
            jax.ShapeDtypeStruct(populations.shape, f32),
            jax.ShapeDtypeStruct((slots * BS, width), f32),
        ),
        in_specs=[ANY, [ANY] * len(cuts), VMEM, VMEM, SMEM],
        out_specs=(VMEM, VMEM),
        scratch_shapes=[
            pltpu.VMEM(populations.shape, f32),
            pltpu.VMEM(populations.shape, f32),
            pltpu.SemaphoreType.DMA((1 + len(cuts),)),
            pltpu.VMEM((slots * BS, width), f32),
            pltpu.VMEM((3, extent_x, extent_y, extent_z), f32),
            pltpu.VMEM((slots * BS, blocks * BS), jnp.bfloat16),
            pltpu.VMEM((2, Q, extent_x + 2, extent_y + 2 * PAD, extent_z), f32),
            pltpu.VMEM((width, blocks * BS), f32),
            pltpu.VMEM((2, 2, 5, extent_y, extent_z), f32),
            pltpu.VMEM((2, 2, 5, extent_y, extent_z), f32),
            pltpu.VMEM((2, 2, 5, extent_x, extent_z), f32),
            pltpu.VMEM((2, 2, 5, extent_x, extent_z), f32),
            pltpu.VMEM((2, 4, 1, extent_z), f32),
            pltpu.VMEM((2, 4, 1, extent_z), f32),
            pltpu.VMEM((slots * BS, width), f32),
            pltpu.VMEM((slots * BS, width), f32),
            pltpu.SemaphoreType.DMA((2, faces)),
            pltpu.SemaphoreType.DMA((2, faces)),
            pltpu.SemaphoreType.DMA((span_x,)),
            pltpu.SemaphoreType.DMA((span_x,)),
            pltpu.SemaphoreType.DMA((span_x,)),
            pltpu.SemaphoreType.DMA((span_x,)),
        ],
        compiler_params=pltpu.CompilerParams(
            collective_id=0, has_side_effects=True, vmem_limit_bytes=48 << 20
        ),
        cost_estimate=pl.CostEstimate(
            flops=100_000_000, bytes_accessed=8_000_000, transcendentals=0
        ),
        name="flow",
    )(whole, list(cuts), outgoing, up, par)
    cell_velocity, flow = pl.pallas_call(
        sample_kernel,
        out_shape=(
            jax.ShapeDtypeStruct(positions.shape, f32),
            jax.ShapeDtypeStruct(populations.shape, f32),
        ),
        in_specs=[VMEM, SMEM, VMEM, ANY],
        out_specs=(VMEM, ANY),
        scratch_shapes=[pltpu.SemaphoreType.DMA],
        compiler_params=pltpu.CompilerParams(vmem_limit_bytes=48 << 20),
        cost_estimate=pl.CostEstimate(
            flops=200_000_000, bytes_accessed=1_000_000, transcendentals=0
        ),
        name="sample",
    )(ret, slot, positions, flow)
    return (flow, cell_velocity.transpose(1, 0, 2))


def solution(mesh):
    placed = (
        P(None, "gx", "gy", None),
        P(None, "gx", "gy", None),
        P(),
        P(),
        P(),
        P(("gx", "gy"), None, None),
        P(),
        P(("gx", "gy")),
        P(("gx", "gy"), None),
        P(("gx", "gy")),
        P(),
    )
    return jax.shard_map(
        functools.partial(body, routes_of(mesh)),
        mesh=mesh,
        in_specs=placed,
        out_specs=(P(None, "gx", "gy", None), P(("gx", "gy"), None, None)),
        check_vma=False,
    )
```
